512 devices in a mesh: dp: 16 (over y_lo, x, core), ctx: 32 (over y_hi, z).
Axes of the slice: x: 4, y: 8 (y_hi: 4, y_lo: 2; y = y_hi * 2 + y_lo), z: 8, core: 2. Of those that a mesh axis runs over, the one named last changes fastest.
Arguments:
- queries: bfloat16 [65536, 512], P(('dp', 'ctx')), may hold values from -16 to 16
- keyvals: bfloat16 [65536, 1024], P(('dp', 'ctx')), may hold values from -4 to 4
- out_weight: bfloat16 [1024, 512], P('ctx'), may hold values from -0.25 to 0.25
- out_grad: bfloat16 [65536, 1024], P(('dp', 'ctx')), may hold values from -24 to 24
- block_lists: int32 [16, 64, 8], P('dp'), may hold values from 0 to 63, as said below
- block_counts: int32 [16, 64], P('dp'), may hold values from 2 to 8, as said below
- seq_lengths: int32 [16], P('dp'), may hold values from 2048 to 4096, as said below
Outputs:
- query_grad: bfloat16 [65536, 512], P(('dp', 'ctx'))
- keyval_grad: bfloat16 [65536, 1024], P(('dp', 'ctx'))
- weight_grad: float32 [1024, 512], P('ctx')
The draws below stay inside these ranges and needn't reach their ends.
Inputs may be any that keep to these rules, and one draw needn't show every extreme that they name: block_lists[s, b, 0] = b. Entry j >= 1 names a block owned by another index of ctx (owner = block // 2); the owners within one list are distinct, and all entries of the query blocks of one owner of ctx that name the same owner name the same block of it. `block_counts`: some query block of every sequence uses all 8 entries. `seq_lengths`: some sequence is full.
All inputs are finite; a program needn't handle non-finite values.
Results may differ from the reference program's by a relative error of at most 0.025.
Values may be sent and summed in bfloat16 or wider, within the bound.
A program may use at most 128 MiB of HBM per device.

```python
import math
import jax
import jax.numpy as jnp
from jax import lax

D = 1024
HEADS = 8
HEAD_DIM = 64
BLK = 64
KPQ = 8
QB_DEV = 2
HD = 512
SEQ = 4096
NQB = 64
TOKENS = 65536
N_DP = 16


def pattern(key):
    base_key = jax.random.fold_in(key, 11)
    key_one, key_two, key_three, key_four, key_five = jax.random.split(base_key, 5)
    owners = NQB // QB_DEV
    requester = jnp.arange(NQB, dtype=jnp.int32) // QB_DEV
    offsets = jax.random.randint(key_one, (N_DP, owners, owners), 0, QB_DEV, dtype=jnp.int32)
    scores = jax.random.randint(key_two, (N_DP, NQB, owners), 0, 2 ** 20, dtype=jnp.int32) * owners
    scores = scores + jnp.arange(owners, dtype=jnp.int32)[None, None, :]
    scores = jnp.where(requester[None, :, None] == jnp.arange(owners, dtype=jnp.int32)[None, None, :], -1, scores)
    chosen = lax.top_k(scores, KPQ - 1)[1].astype(jnp.int32)
    per_row = offsets[:, requester, :]
    picked = jnp.take_along_axis(per_row, chosen, axis=2)
    remote = chosen * QB_DEV + picked
    own_block = jnp.broadcast_to(jnp.arange(NQB, dtype=jnp.int32)[None, :, None], (N_DP, NQB, 1))
    block_list = jnp.concatenate([own_block, remote], axis=2).astype(jnp.int32)
    load_level = jax.random.randint(key_three, (N_DP, owners), 0, 8, dtype=jnp.int32)
    heavy_rank = jax.random.randint(key_four, (N_DP,), 0, owners, dtype=jnp.int32)
    load_level = jnp.where(jnp.arange(owners, dtype=jnp.int32)[None, :] == heavy_rank[:, None], 7, load_level)
    light_count = jax.random.randint(key_five, (N_DP, NQB), 2, KPQ // 2 + 1, dtype=jnp.int32)
    counts = jnp.where(load_level[:, requester] == 7, KPQ, light_count).astype(jnp.int32)
    return (block_list, counts)


def draw_block_lists(key, part):
    return pattern(key)[0]


def draw_block_counts(key, part):
    return pattern(key)[1]


def draw_seq_lengths(key, part):
    base_key = jax.random.fold_in(key, 5)
    key_one, key_two = jax.random.split(base_key, 2)
    lengths_drawn = jax.random.randint(key_one, (N_DP,), SEQ // 2, SEQ + 1, dtype=jnp.int32)
    full_group = jax.random.randint(key_two, (), 0, N_DP, dtype=jnp.int32)
    return jnp.where(jnp.arange(N_DP, dtype=jnp.int32) == full_group, SEQ, lengths_drawn).astype(jnp.int32)


def activations(key):
    base_key = jax.random.fold_in(key, 23)
    key_one, key_two = jax.random.split(base_key, 2)
    width = HEADS * HEAD_DIM
    query_draw = jnp.clip(jax.random.normal(key_one, (TOKENS, width), jnp.float32), -4.0, 4.0)
    keyval_draw = jnp.clip(jax.random.normal(key_two, (TOKENS, 2 * width), jnp.float32), -4.0, 4.0)
    return (query_draw, keyval_draw)


def draw_queries(key, part):
    return activations(key)[0].astype(jnp.bfloat16)


def draw_keyvals(key, part):
    return activations(key)[1].astype(jnp.bfloat16)


def with_spikes(values, own_key, source, target, blocks, factor):
    def block_of(dim):
        return (jnp.arange(values.shape[dim]) // (values.shape[dim] // blocks)).reshape((-1,) + (1,) * (values.ndim - 1 - dim))

    first = jax.random.permutation(own_key, blocks)[block_of(target)]
    far = (block_of(target) + blocks // 2) % blocks
    return jnp.where((block_of(source) == first) | (block_of(source) == far), factor * values, values)


def block_scale(own_key, dims, pieces, least, largest):
    factor_of, own = 1.0, jax.random.fold_in(own_key, 6)
    for axis_at, shards_of in pieces:
        steps = jnp.exp(jax.random.uniform(jax.random.fold_in(own, axis_at), (shards_of,), jnp.float32, least / len(pieces), largest / len(pieces)))
        factor_of = factor_of * jnp.repeat(steps, dims[axis_at] // shards_of).reshape([-1 if axis == axis_at else 1 for axis in range(len(dims))])
    return factor_of


def gaussian(own_key, dims, spread, most, shards=(), kind=jnp.bfloat16):
    drawn = spread * jax.random.normal(own_key, dims, jnp.float32)
    if shards:
        drawn = drawn * block_scale(own_key, dims, shards, -0.22, 0.18)
    return jnp.clip(drawn, -most, most).astype(kind)


def gaussian_with(rng, dims, spread, reach, pieces, heavy, held_as=jnp.bfloat16):
    drawn = spread * jax.random.normal(rng, dims, jnp.float32)
    if pieces:
        drawn = drawn * block_scale(rng, dims, pieces, -0.22, 0.18)
    return jnp.clip(with_spikes(drawn, jax.random.fold_in(rng, 3), *heavy), -reach, reach).astype(held_as)


def setup_inputs(seed: int = 0) -> dict:
    key_of = jax.random.split(jax.random.key(seed), 8)
    return {
        "queries": draw_queries(jax.random.fold_in(key_of[7], 71), 0),
        "keyvals": draw_keyvals(jax.random.fold_in(key_of[7], 71), 0),
        "out_weight": gaussian(key_of[2], (D, HD), HD ** -0.5, 0.25, ((0, 32),)),
        "out_grad": gaussian_with(key_of[3], (TOKENS, D), 1.0, 24.0, ((0, 512),), (0, 1, 512, 6.0)),
        "block_lists": draw_block_lists(jax.random.fold_in(key_of[7], 71), 0),
        "block_counts": draw_block_counts(jax.random.fold_in(key_of[7], 71), 0),
        "seq_lengths": draw_seq_lengths(jax.random.fold_in(key_of[7], 71), 0),
    }


def sequence_grads(query_rows, keyval_rows, grad_rows, full_weight, block_list, counts, length):
    block_total = block_list.shape[0]
    factor = 1.0 / math.sqrt(HEAD_DIM)
    query_pos = jnp.arange(SEQ, dtype=jnp.int32).reshape(block_total, BLK)
    valid_rows = query_pos < length
    query = query_rows.reshape(block_total, BLK, HEADS, HEAD_DIM).astype(jnp.float32)
    gathered = keyval_rows.reshape(block_total, BLK, 2 * HEADS * HEAD_DIM)[block_list]
    gathered = gathered.reshape(block_total, KPQ * BLK, 2, HEADS, HEAD_DIM)
    key_part = gathered[:, :, 0].astype(jnp.float32)
    value_part = gathered[:, :, 1].astype(jnp.float32)
    key_pos = (block_list[:, :, None] * BLK + jnp.arange(BLK, dtype=jnp.int32)[None, None, :]).reshape(block_total, KPQ * BLK)
    active = jnp.repeat(jnp.arange(KPQ, dtype=jnp.int32)[None, :] < counts[:, None], BLK, axis=1)
    allowed = active[:, None, :] & ((key_pos < length)[:, None, :] | (key_pos[:, None, :] == query_pos[:, :, None]))
    scores = jnp.einsum('bihd,bjhd->bhij', query, key_part) * factor
    scores = jnp.where(allowed[:, None], scores, -jnp.inf)
    row_max = lax.optimization_barrier(jnp.max(scores, axis=-1, keepdims=True))
    exponent = jnp.exp(scores - row_max)
    prob_bf16 = (exponent / lax.optimization_barrier(jnp.sum(exponent, axis=-1, keepdims=True))).astype(jnp.bfloat16)
    prob_float = lax.optimization_barrier(prob_bf16).astype(jnp.float32)
    attended = jnp.einsum('bhij,bjhd->bihd', prob_float, value_part)
    attention = (attended * valid_rows[:, :, None, None].astype(jnp.float32)).astype(jnp.bfloat16)
    attention_rows = attention.reshape(SEQ, HEADS * HEAD_DIM)
    attn_full = jnp.dot(grad_rows, full_weight, preferred_element_type=jnp.float32)
    attn_grad = (attn_full * valid_rows.reshape(SEQ, 1).astype(jnp.float32)).astype(jnp.bfloat16)
    grad_heads = attn_grad.reshape(block_total, BLK, HEADS, HEAD_DIM).astype(jnp.float32)
    row_delta = jnp.einsum('bihd,bihd->bhi', grad_heads, attention.astype(jnp.float32))
    prob_grad = jnp.einsum('bihd,bjhd->bhij', grad_heads, value_part)
    score_grad = (prob_float * (prob_grad - row_delta[..., None])).astype(jnp.bfloat16)
    score_float = lax.optimization_barrier(score_grad).astype(jnp.float32)
    query_grad = (jnp.einsum('bhij,bjhd->bihd', score_float, key_part) * factor).astype(jnp.bfloat16)
    key_grad = jnp.einsum('bhij,bihd->bjhd', score_float, query) * factor
    value_grad = jnp.einsum('bhij,bihd->bjhd', prob_float, grad_heads)
    entry_grads = jnp.stack([key_grad, value_grad], axis=2).reshape(block_total * KPQ, BLK * 2 * HEADS * HEAD_DIM)
    summed = jax.ops.segment_sum(entry_grads, block_list.reshape(-1), num_segments=block_total)
    keyval_grad = summed.reshape(SEQ, 2 * HEADS * HEAD_DIM).astype(jnp.bfloat16)
    return (query_grad.reshape(SEQ, HEADS * HEAD_DIM), keyval_grad, attention_rows)

def reference(queries, keyvals, out_weight, out_grad, block_lists, block_counts, seq_lengths):
    query_parts = []
    keyval_parts = []
    weight_sum = jnp.zeros((D, HEADS * HEAD_DIM), jnp.float32)
    for sequence in range(N_DP):
        first_row = sequence * SEQ
        grad_rows = out_grad[first_row:first_row + SEQ]
        query_grad, keyval_grad, attention_rows = sequence_grads(queries[first_row:first_row + SEQ], keyvals[first_row:first_row + SEQ], grad_rows, out_weight, block_lists[sequence], block_counts[sequence], seq_lengths[sequence])
        query_parts.append(query_grad)
        keyval_parts.append(keyval_grad)
        weight_sum = weight_sum + jnp.dot(grad_rows.T, attention_rows, preferred_element_type=jnp.float32)
    weight_grad = weight_sum * (1.0 / math.sqrt(TOKENS))
    return (jnp.concatenate(query_parts, axis=0), jnp.concatenate(keyval_parts, axis=0), weight_grad)
```

```python
import functools
import math

import jax
import jax.numpy as jnp
from jax import lax
from jax.experimental import pallas as pl
from jax.experimental.pallas import tpu as pltpu
from jax.sharding import PartitionSpec as P

HEADS = 8
HEAD_DIM = 64
BLK = 64
KPQ = 8
CTX = 32
PLANE = 8
MESH = pl.DeviceIdType.MESH
BF16 = jnp.bfloat16
F32 = jnp.float32


def to_ctx(src, dst, send, recv, peer):
    return pltpu.make_async_remote_copy(
        src_ref=src, dst_ref=dst, send_sem=send, recv_sem=recv,
        device_id={"ctx": peer}, device_id_type=MESH,
    )


def to_dp(src, dst, send, recv, peer):
    return pltpu.make_async_remote_copy(
        src_ref=src, dst_ref=dst, send_sem=send, recv_sem=recv,
        device_id={"dp": peer}, device_id_type=MESH,
    )


def low_half(shape):
    return lax.broadcasted_iota(jnp.int32, shape, 1) < HEAD_DIM


def pair_up(first, second, which):
    first, second = first.astype(F32), second.astype(F32)
    low = low_half(first.shape)
    if which == 0:
        out = jnp.where(low, first, pltpu.roll(second, HEAD_DIM, 1))
    else:
        out = jnp.where(low, pltpu.roll(first, HEAD_DIM, 1), second)
    return out


def gather_kernel(length_ref, q_ref, kv_ref, w_ref, og_ref, kv_all, qg_all,
                  kv_pack, qg_pack, w_all, w_send, w_recv, s_send, s_recv,
                  kv_send, kv_recv, qg_send, qg_recv):
    dp = lax.axis_index("dp")
    me = lax.axis_index("ctx")
    col, z = me // PLANE, lax.rem(me, PLANE)
    part = lax.rem(dp, PLANE)
    ctx_peers = [lax.rem(me + i, CTX) for i in range(1, CTX)]
    dp_peers = [dp - part + lax.rem(part + i, PLANE) for i in range(1, PLANE)]
    z_peers = [lax.rem(z + i, PLANE) for i in range(1, PLANE)]

    barrier = pltpu.get_barrier_semaphore()
    for peer in ctx_peers:
        pl.semaphore_signal(barrier, inc=1, device_id={"ctx": peer}, device_id_type=MESH)
    for peer in dp_peers:
        pl.semaphore_signal(barrier, inc=1, device_id={"dp": peer}, device_id_type=MESH)

    for head in range(HEADS):
        pair = slice(128 * (head // 2), 128 * (head // 2) + 128)
        vpair = slice(512 + 128 * (head // 2), 512 + 128 * (head // 2) + 128)
        kv_pack[head] = pair_up(kv_ref[:, pair], kv_ref[:, vpair], head % 2).astype(BF16)

    pl.semaphore_wait(barrier, CTX - 1 + PLANE - 1)

    row0 = pl.multiple_of((part // 4) * 16, 16)
    col0 = pl.multiple_of(lax.rem(part, 4) * 128, 128)
    tile = w_ref.at[pl.ds(row0, 16), pl.ds(col0, 128)]
    started = []
    w_copies = []
    for i, peer in enumerate(ctx_peers):
        w_copies.append(to_ctx(tile, w_all.at[part, me], w_send.at[i], w_recv.at[i], peer))
        w_copies[-1].start()
    w_all[part, me] = w_ref[pl.ds(row0, 16), pl.ds(col0, 128)]
    for i, peer in enumerate(ctx_peers):
        copy = to_ctx(kv_pack.at[lax.rem(peer, PLANE)], kv_all.at[me], kv_send.at[i], kv_recv.at[i], peer)
        copy.start()
        started.append(copy)
    kv_all[me] = kv_pack[z]
    for copy in w_copies:
        copy.wait()
    share = []
    for i, peer in enumerate(dp_peers):
        copy = to_dp(w_all.at[part], w_all.at[part], s_send.at[i], s_recv.at[i], peer)
        copy.start()
        share.append(copy)
    for copy in share:
        copy.wait()

    rows = me * 128 + lax.broadcasted_iota(jnp.int32, (128, 1), 0)
    valid = (rows < length_ref[0]).astype(F32)
    out_grad = og_ref[...]
    for c in range(4):
        weight = jnp.stack([w_all[c], w_all[4 + c]], axis=1).reshape(1024, 128)
        grad = jnp.dot(out_grad, weight, preferred_element_type=F32) * valid
        query = q_ref[:, 128 * c:128 * c + 128]
        qg_pack[2 * c] = pair_up(query, grad, 0).astype(BF16)
        qg_pack[2 * c + 1] = pair_up(query, grad, 1).astype(BF16)
    for i, peer in enumerate(z_peers):
        copy = to_ctx(qg_pack.at[peer], qg_all.at[z], qg_send.at[i], qg_recv.at[i], col * PLANE + peer)
        copy.start()
        started.append(copy)
    qg_all[z] = qg_pack[z]
    for copy in started:
        copy.wait()


def attention_kernel(list_ref, count_ref, info_ref, kv_ref, qg_ref, dkv_ref, dqo_ref, total):
    factor = 1.0 / math.sqrt(HEAD_DIM)
    total[...] = jnp.zeros_like(total)
    length = info_ref[0]
    first = info_ref[1]
    lane = lax.broadcasted_iota(jnp.int32, (1, 128), 1)
    low = low_half((BLK, 128))

    def unit(u, carry):
        qg = qg_ref[u].astype(F32)
        left = jnp.concatenate(
            [jnp.where(low, qg * factor, 0.0), jnp.where(low, 0.0, qg)], axis=0
        ).astype(BF16)
        blocks = [list_ref[u, j] for j in range(KPQ)]
        keyval = jnp.concatenate([kv_ref[b] for b in blocks], axis=0)
        both = lax.dot_general(left, keyval, (((1,), (1,)), ((), ())), preferred_element_type=F32)
        count = count_ref[u]
        place = jnp.concatenate(
            [
                jnp.where(lane < BLK, blocks[j] * BLK + lane, blocks[j + 1] * BLK + lane - BLK)
                for j in range(0, KPQ, 2)
            ],
            axis=1,
        )
        entry = lax.broadcasted_iota(jnp.int32, (1, KPQ * BLK), 1) // BLK
        own = (first + u) * BLK + lax.broadcasted_iota(jnp.int32, (BLK, 1), 0)
        allowed = (entry < count) & ((place < length) | (place == own))
        scores = jnp.where(allowed, both[:BLK], -jnp.inf)
        exponent = jnp.exp(scores - jnp.max(scores, axis=1, keepdims=True))
        probs = exponent * (1.0 / jnp.sum(exponent, axis=1, keepdims=True))
        probs16 = probs.astype(BF16)
        probs = probs16.astype(F32)
        prob_grad = both[BLK:]
        delta = jnp.sum(probs * prob_grad, axis=1, keepdims=True)
        score_grad = (probs * (prob_grad - delta)).astype(BF16)
        stacked = jnp.concatenate([score_grad, probs16], axis=0)
        back = jnp.dot(stacked, keyval, preferred_element_type=F32)
        valid = (own < length).astype(F32)
        dqo_ref[u] = jnp.where(low, back[:BLK] * factor, back[BLK:] * valid).astype(BF16)
        grads = lax.dot_general(stacked, left, (((0,), (0,)), ((), ())), preferred_element_type=F32)
        for j in range(KPQ):
            total[blocks[j]] += grads[j * BLK:(j + 1) * BLK]
        return carry

    lax.fori_loop(0, qg_ref.shape[0], unit, 0)
    dkv_ref[...] = total[...].astype(BF16)


def return_kernel(dkv_ref, dqo_ref, dq_out, dkv_out, attn_out, dkv_in, dqo_in,
                  kv_send, kv_recv, q_send, q_recv):
    me = lax.axis_index("ctx")
    col, z = me // PLANE, lax.rem(me, PLANE)
    ctx_peers = [lax.rem(me + i, CTX) for i in range(1, CTX)]
    z_peers = [lax.rem(z + i, PLANE) for i in range(1, PLANE)]
    barrier = pltpu.get_barrier_semaphore()
    for peer in ctx_peers:
        pl.semaphore_signal(barrier, inc=1, device_id={"ctx": peer}, device_id_type=MESH)
    pl.semaphore_wait(barrier, CTX - 1)
    q_copies, kv_copies = [], []
    for i, peer in enumerate(z_peers):
        copy = to_ctx(dqo_ref.at[peer], dqo_in.at[z], q_send.at[i], q_recv.at[i], col * PLANE + peer)
        copy.start()
        q_copies.append(copy)
    for i, peer in enumerate(ctx_peers):
        copy = to_ctx(dkv_ref.at[peer], dkv_in.at[me], kv_send.at[i], kv_recv.at[i], peer)
        copy.start()
        kv_copies.append(copy)
    dqo_in[z] = dqo_ref[z]
    dkv_in[me] = dkv_ref[me]
    for copy in q_copies:
        copy.wait()
    for c in range(4):
        even, odd = dqo_in[2 * c], dqo_in[2 * c + 1]
        cols = slice(128 * c, 128 * c + 128)
        dq_out[:, cols] = pair_up(even, odd, 0).astype(BF16)
        attn_out[:, cols] = pair_up(even, odd, 1).astype(BF16)
    for copy in kv_copies:
        copy.wait()
    for c in range(4):
        sums = []
        for head in (2 * c, 2 * c + 1):
            sums.append(sum(dkv_in[y * PLANE + head].astype(F32) for y in range(CTX // PLANE)))
        dkv_out[:, 128 * c:128 * c + 128] = pair_up(sums[0], sums[1], 0).astype(BF16)
        dkv_out[:, 512 + 128 * c:512 + 128 * c + 128] = pair_up(sums[0], sums[1], 1).astype(BF16)


def vmem(n):
    return [pl.BlockSpec(memory_space=pltpu.VMEM)] * n


def per_device(queries, keyvals, out_weight, out_grad, block_lists, block_counts, seq_lengths):
    me = lax.axis_index("ctx")
    dma = pltpu.SemaphoreType.DMA
    smem = pl.BlockSpec(memory_space=pltpu.SMEM)
    kv_all, qg_all = pl.pallas_call(
        gather_kernel,
        out_shape=(
            jax.ShapeDtypeStruct((CTX, 128, 128), BF16),
            jax.ShapeDtypeStruct((PLANE, 128, 128), BF16),
        ),
        in_specs=[smem] + vmem(4),
        out_specs=tuple(vmem(2)),
        scratch_shapes=[
            pltpu.VMEM((HEADS, 128, 128), BF16),
            pltpu.VMEM((HEADS, 128, 128), BF16),
            pltpu.VMEM((PLANE, CTX, 16, 128), BF16),
            dma((CTX - 1,)), dma((CTX - 1,)),
            dma((PLANE - 1,)), dma((PLANE - 1,)),
            dma((CTX - 1,)), dma((CTX - 1,)),
            dma((PLANE - 1,)), dma((PLANE - 1,)),
        ],
        compiler_params=pltpu.CompilerParams(
            collective_id=0, has_side_effects=True, vmem_limit_bytes=32 * 2**20
        ),
        name="gather",
    )(seq_lengths, queries, keyvals, out_weight, out_grad)

    first = (me // PLANE) * 16
    mine = lax.dynamic_slice_in_dim(block_lists[0], first, 16, 0)
    counts = lax.dynamic_slice_in_dim(block_counts[0], first, 16, 0)
    info = jnp.stack([seq_lengths[0], first])
    dkv, dqo = pl.pallas_call(
        attention_kernel,
        out_shape=(
            jax.ShapeDtypeStruct((64, BLK, 128), BF16),
            jax.ShapeDtypeStruct((16, BLK, 128), BF16),
        ),
        in_specs=[smem] * 3 + vmem(2),
        out_specs=tuple(vmem(2)),
        scratch_shapes=[pltpu.VMEM((64, BLK, 128), F32)],
        compiler_params=pltpu.CompilerParams(vmem_limit_bytes=32 * 2**20),
        name="attention",
    )(mine, counts, info, kv_all.reshape(64, BLK, 128), qg_all.reshape(16, BLK, 128))

    query_grad, keyval_grad, attention_rows = pl.pallas_call(
        return_kernel,
        out_shape=(
            jax.ShapeDtypeStruct((128, 512), BF16),
            jax.ShapeDtypeStruct((128, 1024), BF16),
            jax.ShapeDtypeStruct((128, 512), BF16),
        ),
        in_specs=vmem(2),
        out_specs=tuple(vmem(3)),
        scratch_shapes=[
            pltpu.VMEM((CTX, 128, 128), BF16),
            pltpu.VMEM((PLANE, 128, 128), BF16),
            dma((CTX - 1,)), dma((CTX - 1,)),
            dma((PLANE - 1,)), dma((PLANE - 1,)),
        ],
        compiler_params=pltpu.CompilerParams(
            collective_id=1, has_side_effects=True, vmem_limit_bytes=32 * 2**20
        ),
        name="giveback",
    )(dkv.reshape(CTX, 128, 128), dqo.reshape(PLANE, 128, 128))

    groups = lax.axis_size("dp")
    scaling = 1.0 / math.sqrt(128 * CTX * groups)
    shard_sum = lax.psum_scatter(
        (
            lax.dot_general(
                out_grad, attention_rows, (((0,), (0,)), ((), ())), preferred_element_type=F32
            )
            * scaling
        ).astype(BF16),
        "ctx",
        scatter_dimension=0,
        tiled=True,
    )
    weight_grad = lax.psum(shard_sum, "dp").astype(F32)
    return (query_grad, keyval_grad, weight_grad)


def solution(mesh):
    placed = (
        P(("dp", "ctx"), None),
        P(("dp", "ctx"), None),
        P("ctx", None),
        P(("dp", "ctx"), None),
        P("dp", None, None),
        P("dp", None),
        P("dp"),
    )
    return jax.shard_map(
        per_device,
        mesh=mesh,
        in_specs=placed,
        out_specs=(P(("dp", "ctx"), None), P(("dp", "ctx"), None), P("ctx", None)),
        check_vma=False,
    )
```

```python
import math

import jax
import jax.numpy as jnp
from jax import lax
from jax.experimental import pallas as pl
from jax.experimental.pallas import tpu as pltpu
from jax.sharding import PartitionSpec as P

HEADS = 8
HEAD_DIM = 64
BLK = 64
KPQ = 8
NQB = 64
CTX = 32
DP = 16
PLANE = 8
UNITS = 16
ENTRIES = UNITS * KPQ
FACTOR = 1.0 / math.sqrt(HEAD_DIM)
WG_SCALE = 1.0 / math.sqrt(128 * CTX * DP)
MESH = pl.DeviceIdType.MESH
BF16 = jnp.bfloat16
F32 = jnp.float32

T_LIST = 0
T_PERM = T_LIST + ENTRIES
T_SAME = T_PERM + ENTRIES
T_LAST = T_SAME + ENTRIES
T_COUNT = T_LAST + NQB
T_LENGTH = T_COUNT + UNITS


def low_half(shape):
    return lax.broadcasted_iota(jnp.int32, shape, 1) < HEAD_DIM


def pair_up(first, second, which):
    first, second = first.astype(F32), second.astype(F32)
    low = low_half(first.shape)
    if which == 0:
        return jnp.where(low, first, pltpu.roll(second, HEAD_DIM, 1))
    return jnp.where(low, pltpu.roll(first, HEAD_DIM, 1), second)


def dot(a, b, dims=((1,), (0,))):
    return lax.dot_general(a, b, (dims, ((), ())), preferred_element_type=F32)


def remote(src, dst, send, recv, **where):
    return pltpu.make_async_remote_copy(
        src_ref=src, dst_ref=dst, send_sem=send, recv_sem=recv,
        device_id=where, device_id_type=MESH,
    )


def body(tab, q_hbm, kv_hbm, w_hbm, og_hbm, dq_out, dkv_out, wg_out,
         q_ref, kv_ref, w_ref, w_tile, w_all, og_all, og_t, q_pack, q_all, kv_pack, kv_all,
         g_pack, g_all, p_all, o_pack, o_all, dq_pack, dq_all, entry_grads, sums,
         dkv_pack, dkv_in, wg_pack, wg_in, wg_last, wg_all,
         in_sem, w_s, w_r, og_s, og_r, oc_s, oc_r, q_s, q_r, kv_s, kv_r, g_s, g_r,
         o_s, o_r, dq_s, dq_r, dkv_s, dkv_r, b_s, b_r, c_s, c_r):
    dp = lax.axis_index("dp")
    me = lax.axis_index("ctx")
    col, z = me // PLANE, lax.rem(me, PLANE)
    part = lax.rem(dp, PLANE)
    base = dp - part
    x, core = part // 2, lax.rem(part, 2)
    partner = base + 2 * x + 1 - core
    ctx_peers = [lax.rem(me + i, CTX) for i in range(1, CTX)]
    dp_peers = [lax.rem(dp + i, DP) for i in range(1, DP)]
    z_peers = [lax.rem(z + i, PLANE) for i in range(1, PLANE)]
    x_peers = [lax.rem(x + i, 4) for i in range(1, 4)]
    here = part == z

    loads = [
        pltpu.make_async_copy(w_hbm, w_ref, in_sem.at[0]),
        pltpu.make_async_copy(og_hbm, og_all.at[part], in_sem.at[1]),
        pltpu.make_async_copy(q_hbm, q_ref, in_sem.at[2]),
        pltpu.make_async_copy(kv_hbm, kv_ref, in_sem.at[3]),
    ]
    for copy in loads:
        copy.start()

    barrier = pltpu.get_barrier_semaphore()

    def greet(**where):
        pl.semaphore_signal(barrier, inc=1, device_id=where, device_id_type=MESH)

    for peer in ctx_peers:
        greet(ctx=peer)
    for peer in dp_peers:
        greet(dp=peer)
    for i in range(1, PLANE):
        greet(dp=base + z, ctx=col * PLANE + lax.rem(z + i, PLANE))
        greet(dp=base + lax.rem(part + i, PLANE), ctx=col * PLANE + part)

    @pl.when(jnp.logical_not(here))
    def _():
        greet(dp=base + z, ctx=me)
        greet(dp=dp, ctx=col * PLANE + part)

    low16 = low_half((16, 128))
    low = low_half((BLK, 128))
    loads[0].wait()
    pair = w_ref[:, pl.ds(pl.multiple_of(128 * (part // 2), 128), 128)]
    odd = (lax.rem(part, 2) == 1).astype(F32)
    tile = pair_up(pair[:16], pair[16:], 0) * (1.0 - odd) + pair_up(pair[:16], pair[16:], 1) * odd
    w_tile[...] = tile.astype(BF16)
    w_all[me] = tile.astype(BF16)
    loads[2].wait()
    for head in range(HEADS):
        cols = slice(128 * (head // 2), 128 * (head // 2) + 128)
        q_pack[head] = pair_up(q_ref[:BLK, cols], q_ref[BLK:, cols], head % 2).astype(BF16)
    loads[3].wait()
    for head in range(HEADS):
        first = 128 * (head // 2)
        for half in range(2):
            rows = slice(BLK * half, BLK * half + BLK)
            kv_pack[head, half] = pair_up(
                kv_ref[rows, first:first + 128], kv_ref[rows, 512 + first:640 + first], head % 2
            ).astype(BF16)
    loads[1].wait()

    barrier_count = CTX - 1 + DP - 1 + 2 * (PLANE - 1) + jnp.where(here, 0, 2)
    pl.semaphore_wait(barrier, barrier_count)

    w_copies, og_copies, og_core, q_copies, kv_copies = [], [], [], [], []
    for i, peer in enumerate(ctx_peers):
        w_copies.append(remote(w_tile, w_all.at[me], w_s.at[i], w_r.at[i], ctx=peer))
    for i, peer in enumerate(x_peers):
        mine = og_all.at[part]
        og_copies.append(
            remote(mine, mine, og_s.at[i], og_r.at[i], dp=base + 2 * peer + core)
        )
    og_core.append(remote(og_all.at[part], og_all.at[part], oc_s.at[3], oc_r.at[3], dp=partner))
    for i, peer in enumerate(z_peers):
        q_copies.append(
            remote(q_pack.at[peer], q_all.at[z], q_s.at[i], q_r.at[i], ctx=col * PLANE + peer)
        )
    for i, peer in enumerate(ctx_peers):
        kv_copies.append(
            remote(kv_pack.at[lax.rem(peer, PLANE)], kv_all.at[pl.ds(2 * me, 2)],
                   kv_s.at[i], kv_r.at[i], ctx=peer)
        )
    for copy in w_copies + og_copies + og_core + q_copies + kv_copies:
        copy.start()
    q_all[z] = q_pack[z]
    kv_all[pl.ds(2 * me, 2)] = kv_pack[z]

    for i in range(3):
        og_copies[i].wait_recv()
        slot = 2 * lax.rem(x + 3 - i, 4) + core
        copy = remote(og_all.at[slot], og_all.at[slot], oc_s.at[i], oc_r.at[i], dp=partner)
        copy.start()
        og_core.append(copy)
    for copy in w_copies:
        copy.wait()
    for copy in og_core:
        copy.wait_recv()

    weight = w_all[...].reshape(CTX, 1, 16, 128)
    none = jnp.zeros_like(weight)
    low4 = lax.broadcasted_iota(jnp.int32, weight.shape, 3) < HEAD_DIM
    weight = jnp.concatenate(
        [jnp.where(low4, weight, none), jnp.where(low4, none, weight)], axis=1
    ).reshape(CTX * 32, 128)
    for s in range(PLANE):
        grad = dot(og_all[s], weight)
        grad = grad + pltpu.roll(grad, HEAD_DIM, 1)
        g_pack[s] = jnp.where(low, grad[:BLK], grad[BLK:]).astype(BF16)
    g_copies = []
    for i in range(PLANE):
        peer = lax.rem(part + i, PLANE)
        copy = remote(g_pack.at[peer], g_all.at[z], g_s.at[i], g_r.at[z],
                      dp=base + peer, ctx=col * PLANE + part)
        g_copies.append(copy)
        if i:
            copy.start()
        else:
            pl.when(jnp.logical_not(here))(copy.start)

            @pl.when(here)
            def _():
                g_all[z] = g_pack[part]

    for s in range(PLANE):
        og_t[:, 128 * s:128 * s + 128] = og_all[s].T
    for copy in q_copies + kv_copies:
        copy.wait_recv()

    length = tab[T_LENGTH]
    lane = lax.broadcasted_iota(jnp.int32, (1, 128), 1)
    row = lax.broadcasted_iota(jnp.int32, (BLK, 1), 0)
    entry = lax.broadcasted_iota(jnp.int32, (1, KPQ * BLK), 1) // BLK

    def listed(u):
        blocks = [tab[T_LIST + u * KPQ + j] for j in range(KPQ)]
        return blocks, jnp.concatenate([kv_all[b] for b in blocks], axis=0)

    def forward(zp, carry):
        query = q_all[zp].astype(F32) * FACTOR
        outs = []
        for p in range(2):
            u = 2 * zp + p
            blocks, keyval = listed(u)
            left = query if p == 0 else pltpu.roll(query, HEAD_DIM, 1)
            scores = dot(jnp.where(low, left, 0.0).astype(BF16), keyval, ((1,), (1,)))
            place = jnp.concatenate(
                [
                    jnp.where(lane < BLK, blocks[j] * BLK + lane, blocks[j + 1] * BLK + lane - BLK)
                    for j in range(0, KPQ, 2)
                ],
                axis=1,
            )
            own = (col * UNITS + u) * BLK + row
            allowed = (entry < tab[T_COUNT + u]) & ((place < length) | (place == own))
            scores = jnp.where(allowed, scores, -jnp.inf)
            exponent = jnp.exp(scores - jnp.max(scores, axis=1, keepdims=True))
            probs = exponent * (1.0 / jnp.sum(exponent, axis=1, keepdims=True))
            probs = probs.astype(BF16)
            p_all[u] = probs
            outs.append(dot(probs, keyval) * (own < length).astype(F32))
        o_pack[zp] = pair_up(outs[0], outs[1], 1).astype(BF16)
        return carry

    lax.fori_loop(0, PLANE, forward, 0)

    o_copies = []
    for i in range(PLANE):
        peer = lax.rem(z + i, PLANE)
        copy = remote(o_pack.at[peer], o_all.at[part], o_s.at[i], o_r.at[part],
                      dp=base + z, ctx=col * PLANE + peer)
        o_copies.append(copy)
        if i:
            copy.start()
        else:
            pl.when(jnp.logical_not(here))(copy.start)

            @pl.when(here)
            def _():
                o_all[part] = o_pack[z]

    def arrived(dst, sem):
        remote(dst, dst, sem, sem, dp=dp, ctx=me).wait_recv()

    for i in range(1, PLANE):
        slot = lax.rem(z + i, PLANE)
        arrived(g_all.at[slot], g_r.at[slot])

    @pl.when(jnp.logical_not(here))
    def _():
        arrived(g_all.at[z], g_r.at[z])

    def backward(zp, carry):
        query = q_all[zp].astype(F32) * FACTOR
        grads = g_all[zp].astype(F32)
        outs = []
        for p in range(2):
            u = 2 * zp + p
            _, keyval = listed(u)
            valid = ((col * UNITS + u) * BLK + row < length).astype(F32)
            if p == 0:
                top, bottom = query, pltpu.roll(grads, HEAD_DIM, 1)
            else:
                top, bottom = pltpu.roll(query, HEAD_DIM, 1), grads
            top = jnp.where(low, top, 0.0).astype(BF16)
            bottom = jnp.where(low, 0.0, bottom * valid).astype(BF16)
            prob_grad = dot(bottom, keyval, ((1,), (1,)))
            probs16 = p_all[u]
            probs = probs16.astype(F32)
            delta = jnp.sum(probs * prob_grad, axis=1, keepdims=True)
            score_grad = (probs * (prob_grad - delta)).astype(BF16)
            outs.append(dot(score_grad, keyval) * FACTOR)
            stacked = jnp.concatenate([score_grad, probs16], axis=0)
            grad = dot(stacked, jnp.concatenate([top, bottom], axis=0), ((0,), (0,)))
            for j in range(KPQ):
                entry_grads[u * KPQ + j] = grad[j * BLK:(j + 1) * BLK]
        dq_pack[zp] = pair_up(outs[0], outs[1], 0).astype(BF16)
        return carry

    lax.fori_loop(0, PLANE, backward, 0)

    dq_copies = []
    for i, peer in enumerate(z_peers):
        copy = remote(dq_pack.at[peer], dq_all.at[z], dq_s.at[i], dq_r.at[i], ctx=col * PLANE + peer)
        copy.start()
        dq_copies.append(copy)
    dq_all[z] = dq_pack[z]

    for i in range(1, PLANE):
        slot = lax.rem(part + i, PLANE)
        arrived(o_all.at[slot], o_r.at[slot])

    @pl.when(jnp.logical_not(here))
    def _():
        arrived(o_all.at[part], o_r.at[part])

    attention = o_all[...].reshape(PLANE, 1, BLK, 128)
    none = jnp.zeros_like(attention)
    low4 = lax.broadcasted_iota(jnp.int32, attention.shape, 3) < HEAD_DIM
    attention = jnp.concatenate(
        [jnp.where(low4, attention, none), jnp.where(low4, none, attention)], axis=1
    ).reshape(PLANE * 128, 128)
    for c in range(0, CTX, 8):
        grad = dot(og_t[32 * c:32 * c + 256], attention)
        grad = ((grad + pltpu.roll(grad, HEAD_DIM, 1)) * WG_SCALE).reshape(8, 2, 16, 128)
        for k in range(8):
            wg_pack[c + k] = jnp.where(low16, grad[k, 0], grad[k, 1]).astype(BF16)
    b_copies = []
    for i, peer in enumerate(ctx_peers):
        copy = remote(wg_pack.at[peer], wg_in.at[me], b_s.at[i], b_r.at[i], ctx=peer)
        copy.start()
        b_copies.append(copy)
    wg_in[me] = wg_pack[me]

    sums[ENTRIES] = jnp.zeros((BLK, 128), F32)

    def accumulate(t, total):
        total = entry_grads[tab[T_PERM + t]] + total * tab[T_SAME + t].astype(F32)
        sums[t] = total
        return total

    lax.fori_loop(0, ENTRIES, accumulate, jnp.zeros((BLK, 128), F32), unroll=4)

    def pack(c, carry):
        for half in range(2):
            dkv_pack[c, half] = sums[tab[T_LAST + 2 * c + half]].astype(BF16)
        return carry

    lax.fori_loop(0, CTX, pack, 0, unroll=2)
    dkv_copies = []
    for i, peer in enumerate(ctx_peers):
        copy = remote(dkv_pack.at[peer], dkv_in.at[me], dkv_s.at[i], dkv_r.at[i], ctx=peer)
        copy.start()
        dkv_copies.append(copy)
    dkv_in[me] = dkv_pack[me]

    for copy in b_copies:
        copy.wait()
    wg_last[...] = sum(wg_in[i].astype(F32) for i in range(CTX)).astype(BF16)
    c_copies = []
    for i, peer in enumerate(dp_peers):
        copy = remote(wg_last, wg_all.at[dp], c_s.at[i], c_r.at[i], dp=peer)
        copy.start()
        c_copies.append(copy)
    wg_all[dp] = wg_last[...]

    for copy in dq_copies:
        copy.wait()
    for c in range(4):
        for half in range(2):
            dq_out[BLK * half:BLK * half + BLK, 128 * c:128 * c + 128] = pair_up(
                dq_all[2 * c], dq_all[2 * c + 1], half
            ).astype(BF16)

    for copy in c_copies:
        copy.wait()
    for c in range(4):
        even = wg_all[2 * c].astype(F32) + wg_all[PLANE + 2 * c].astype(F32)
        odd_ = wg_all[2 * c + 1].astype(F32) + wg_all[PLANE + 2 * c + 1].astype(F32)
        for half in range(2):
            wg_out[16 * half:16 * half + 16, 128 * c:128 * c + 128] = pair_up(even, odd_, half)

    for copy in dkv_copies:
        copy.wait()
    for c in range(4):
        for half in range(2):
            rows = slice(BLK * half, BLK * half + BLK)
            even, odd_ = [
                sum(dkv_in[y * PLANE + head, half].astype(F32) for y in range(CTX // PLANE))
                for head in (2 * c, 2 * c + 1)
            ]
            dkv_out[rows, 128 * c:128 * c + 128] = pair_up(even, odd_, 0).astype(BF16)
            dkv_out[rows, 512 + 128 * c:640 + 128 * c] = pair_up(even, odd_, 1).astype(BF16)

    for copy in og_copies + og_core + q_copies + kv_copies + g_copies[1:] + o_copies[1:]:
        copy.wait_send()

    @pl.when(jnp.logical_not(here))
    def _():
        g_copies[0].wait_send()
        o_copies[0].wait_send()


def table(block_list, counts, length, first):
    mine = lax.dynamic_slice_in_dim(block_list, first, UNITS, 0).reshape(ENTRIES)
    ids = jnp.arange(ENTRIES, dtype=jnp.int32)
    key = mine * ENTRIES + ids
    place = jnp.sum((key[None, :] < key[:, None]).astype(jnp.int32), axis=1)
    at = place[None, :] == ids[:, None]
    perm = jnp.sum(jnp.where(at, ids[None, :], 0), axis=1)
    same = (mine[None, :] == mine[:, None]) & (ids[None, :] < ids[:, None])
    later = jnp.max(same.astype(jnp.int32), axis=1)
    go_on = jnp.sum(jnp.where(at, later[None, :], 0), axis=1)
    blocks = jnp.arange(NQB, dtype=jnp.int32)
    upto = jnp.sum((mine[None, :] <= blocks[:, None]).astype(jnp.int32), axis=1)
    named = jnp.max((mine[None, :] == blocks[:, None]).astype(jnp.int32), axis=1)
    last = jnp.where(named > 0, upto - 1, ENTRIES)
    mine_counts = lax.dynamic_slice_in_dim(counts, first, UNITS, 0)
    return jnp.concatenate([mine, perm, go_on, last, mine_counts, length])


def per_device(queries, keyvals, out_weight, out_grad, block_lists, block_counts, seq_lengths):
    first = (lax.axis_index("ctx") // PLANE) * UNITS
    tab = table(block_lists[0], block_counts[0], seq_lengths, first)
    dma = pltpu.SemaphoreType.DMA
    vm = pltpu.VMEM
    any_space = pl.BlockSpec(memory_space=pl.ANY)
    pairs = [CTX - 1, 3, 4, PLANE - 1, CTX - 1, PLANE, PLANE, PLANE - 1, CTX - 1, CTX - 1, DP - 1]
    return pl.pallas_call(
        body,
        out_shape=(
            jax.ShapeDtypeStruct((128, 512), BF16),
            jax.ShapeDtypeStruct((128, 1024), BF16),
            jax.ShapeDtypeStruct((32, 512), F32),
        ),
        in_specs=[pl.BlockSpec(memory_space=pltpu.SMEM)] + [any_space] * 4,
        out_specs=tuple([pl.BlockSpec(memory_space=pltpu.VMEM)] * 3),
        scratch_shapes=[
            vm((128, 512), BF16), vm((128, 1024), BF16), vm((32, 512), BF16),
            vm((16, 128), BF16), vm((CTX, 16, 128), BF16),
            vm((PLANE, 128, 1024), BF16), vm((1024, 1024), BF16),
            vm((HEADS, BLK, 128), BF16), vm((PLANE, BLK, 128), BF16),
            vm((HEADS, 2, BLK, 128), BF16), vm((NQB, BLK, 128), BF16),
            vm((PLANE, BLK, 128), BF16), vm((PLANE, BLK, 128), BF16),
            vm((UNITS, BLK, KPQ * BLK), BF16),
            vm((PLANE, BLK, 128), BF16), vm((PLANE, BLK, 128), BF16),
            vm((PLANE, BLK, 128), BF16), vm((PLANE, BLK, 128), BF16),
            vm((ENTRIES, BLK, 128), F32), vm((ENTRIES + 1, BLK, 128), F32),
            vm((CTX, 2, BLK, 128), BF16), vm((CTX, 2, BLK, 128), BF16),
            vm((CTX, 16, 128), BF16), vm((CTX, 16, 128), BF16),
            vm((16, 128), BF16), vm((DP, 16, 128), BF16),
            dma((4,)),
        ] + [dma((n,)) for n in pairs for _ in range(2)],
        compiler_params=pltpu.CompilerParams(
            collective_id=0, has_side_effects=True, vmem_limit_bytes=48 * 2**20
        ),
        name="attention_step",
    )(tab, queries, keyvals, out_weight, out_grad)


def solution(mesh):
    placed = (
        P(("dp", "ctx"), None),
        P(("dp", "ctx"), None),
        P("ctx", None),
        P(("dp", "ctx"), None),
        P("dp", None, None),
        P("dp", None),
        P("dp"),
    )
    return jax.shard_map(
        per_device,
        mesh=mesh,
        in_specs=placed,
        out_specs=(P(("dp", "ctx"), None), P(("dp", "ctx"), None), P("ctx", None)),
        check_vma=False,
    )
```

```python
import math

import jax
import jax.numpy as jnp
from jax import lax
from jax.experimental import pallas as pl
from jax.experimental.pallas import tpu as pltpu
from jax.sharding import PartitionSpec as P

HEADS = 8
HEAD_DIM = 64
BLK = 64
KPQ = 8
NQB = 64
CTX = 32
COLS = 4
LAG = 2
DP = 16
PLANE = 8
UNITS = 16
ENTRIES = UNITS * KPQ
FACTOR = 1.0 / math.sqrt(HEAD_DIM)
WG_SCALE = 1.0 / math.sqrt(128 * CTX * DP)
MESH = pl.DeviceIdType.MESH
BF16 = jnp.bfloat16
F32 = jnp.float32

T_LIST = 0
T_PERM = T_LIST + ENTRIES
T_SAME = T_PERM + ENTRIES
T_LAST = T_SAME + ENTRIES
T_COUNT = T_LAST + NQB
T_LENGTH = T_COUNT + UNITS


def low_half(shape):
    return lax.broadcasted_iota(jnp.int32, shape, 1) < HEAD_DIM


def pair_up(first, second, which):
    first, second = first.astype(F32), second.astype(F32)
    low = low_half(first.shape)
    if which == 0:
        return jnp.where(low, first, pltpu.roll(second, HEAD_DIM, 1))
    return jnp.where(low, pltpu.roll(first, HEAD_DIM, 1), second)


def dot(a, b, dims=((1,), (0,))):
    return lax.dot_general(a, b, (dims, ((), ())), preferred_element_type=F32)


def remote(src, dst, send, recv, **where):
    return pltpu.make_async_remote_copy(
        src_ref=src, dst_ref=dst, send_sem=send, recv_sem=recv,
        device_id=where, device_id_type=MESH,
    )


def body(tab, q_hbm, kv_hbm, w_hbm, og_hbm, dq_out, dkv_out, wg_out,
         q_ref, kv_ref, w_ref, w_tile, w_all, og_all, og_t, q_pack, q_all, kv_pack, kv_all,
         g_pack, g_all, p_all, o_pack, o_all, dq_pack, dq_all, entry_grads, sums,
         dkv_pack, dkv_y, dkv_z, dkv_in, wg_pack, wg_in, wg_mid, wg_col, wg_last, wg_all,
         in_sem, w_s, w_r, wy_s, wy_r, og_s, og_r, oc_s, oc_r, q_s, q_r, kv_s, kv_r, kvy_s, kvy_r,
         g_s, g_r, o_s, o_r, dq_s, dq_r, dkvy_s, dkvy_r, dkv_s, dkv_r, b_s, b_r, by_s, by_r,
         c_s, c_r):
    dp = lax.axis_index("dp")
    me = lax.axis_index("ctx")
    col, z = me // PLANE, lax.rem(me, PLANE)
    part = lax.rem(dp, PLANE)
    base = dp - part
    x, core = part // 2, lax.rem(part, 2)
    partner = base + 2 * x + 1 - core
    col_peers = [lax.rem(col + i, COLS) for i in range(1, COLS)]
    dp_peers = [lax.rem(dp + i, DP) for i in range(1, DP)]
    z_peers = [lax.rem(z + i, PLANE) for i in range(1, PLANE)]
    x_peers = [lax.rem(x + i, 4) for i in range(1, 4)]
    here = part == z

    loads = [
        pltpu.make_async_copy(w_hbm, w_ref, in_sem.at[0]),
        pltpu.make_async_copy(og_hbm, og_all.at[part], in_sem.at[1]),
        pltpu.make_async_copy(q_hbm, q_ref, in_sem.at[2]),
        pltpu.make_async_copy(kv_hbm, kv_ref, in_sem.at[3]),
    ]
    for copy in loads:
        copy.start()

    barrier = pltpu.get_barrier_semaphore()

    def greet(**where):
        pl.semaphore_signal(barrier, inc=1, device_id=where, device_id_type=MESH)

    for peer in z_peers:
        greet(ctx=col * PLANE + peer)
    for peer in col_peers:
        greet(ctx=peer * PLANE + z)
    for peer in dp_peers:
        greet(dp=peer)
    for i in range(1, PLANE):
        other = lax.rem(part + i, PLANE)
        greet(dp=base + other, ctx=col * PLANE + part)
        greet(dp=base + other, ctx=col * PLANE + lax.rem(z + PLANE - other, PLANE))
    stays = part == 0

    @pl.when(jnp.logical_not(here))
    def _():
        greet(dp=dp, ctx=col * PLANE + part)

    @pl.when(jnp.logical_not(stays))
    def _():
        greet(dp=dp, ctx=col * PLANE + lax.rem(z + PLANE - part, PLANE))

    low16 = low_half((16, 128))
    low = low_half((BLK, 128))
    loads[0].wait()
    for head in range(HEADS):
        cols = slice(128 * (head // 2), 128 * (head // 2) + 128)
        w_tile[head] = pair_up(w_ref[:16, cols], w_ref[16:, cols], head % 2).astype(BF16)
    w_all[me] = w_tile[lax.rem(part + z, HEADS)]
    loads[2].wait()
    for head in range(HEADS):
        cols = slice(128 * (head // 2), 128 * (head // 2) + 128)
        q_pack[head] = pair_up(q_ref[:BLK, cols], q_ref[BLK:, cols], head % 2).astype(BF16)
    loads[3].wait()
    for head in range(HEADS):
        first = 128 * (head // 2)
        for half in range(2):
            rows = slice(BLK * half, BLK * half + BLK)
            kv_pack[head, half] = pair_up(
                kv_ref[rows, first:first + 128], kv_ref[rows, 512 + first:640 + first], head % 2
            ).astype(BF16)
    loads[1].wait()

    barrier_count = PLANE - 1 + COLS - 1 + DP - 1 + 2 * (PLANE - 1)
    barrier_count = barrier_count + jnp.where(here, 0, 1) + jnp.where(stays, 0, 1)
    pl.semaphore_wait(barrier, barrier_count)

    w_copies, wy_copies, og_copies, og_core, q_copies, kv_copies, kvy_copies = [], [], [], [], [], [], []

    def rank_rows(ref, rank):
        return ref.at[pl.ds(2 * rank, 2)]

    right, left = lax.rem(col + 1, COLS), lax.rem(col + COLS - 1, COLS)
    to_right, to_left = [], []

    def pass_on(rank, n, to, kept):
        rows = rank_rows(kv_all, rank)
        copy = remote(rows, rows, kvy_s.at[n], kvy_r.at[n], ctx=to * PLANE + z)
        copy.start()
        kept.append(copy)
        kvy_copies.append(copy)

    def down_column(i):
        rank = col * PLANE + lax.rem(z + PLANE - i, PLANE)
        pass_on(rank, 2 * i, right, to_right)
        pass_on(rank, 2 * i + 1, left, to_left)

    def across_column(i):
        at = lax.rem(z + PLANE - i, PLANE)
        if i % 2 == 0:
            to_right[i].wait_recv()
            pass_on(left * PLANE + at, 2 * PLANE + i, right, far)
        else:
            to_left[i].wait_recv()
            pass_on(right * PLANE + at, 2 * PLANE + i, left, far)

    far = []
    for i, peer in enumerate(z_peers):
        w_copies.append(
            remote(w_tile.at[lax.rem(part + peer, HEADS)], w_all.at[me], w_s.at[i], w_r.at[i],
                   ctx=col * PLANE + peer)
        )
        w_copies[i].start()
    mine = og_all.at[part]
    for i, peer in enumerate(x_peers):
        og_copies.append(remote(mine, mine, og_s.at[i], og_r.at[i], dp=base + 2 * peer + core))
        og_copies[i].start()
    for i, peer in enumerate(z_peers):
        copy = remote(kv_pack.at[peer], rank_rows(kv_all, me), kv_s.at[i], kv_r.at[i],
                      ctx=col * PLANE + peer)
        copy.start()
        kv_copies.append(copy)
    kv_all[pl.ds(2 * me, 2)] = kv_pack[z]
    down_column(0)
    og_core.append(remote(mine, mine, oc_s.at[3], oc_r.at[3], dp=partner))
    og_core[0].start()
    for copy in w_copies:
        copy.wait()
    for j, peer in enumerate(col_peers):
        rows = w_all.at[pl.ds(col * PLANE, PLANE)]
        copy = remote(rows, rows, wy_s.at[j], wy_r.at[j], ctx=peer * PLANE + z)
        copy.start()
        wy_copies.append(copy)
    for i, peer in enumerate(z_peers):
        q_copies.append(
            remote(q_pack.at[peer], q_all.at[z], q_s.at[i], q_r.at[i], ctx=col * PLANE + peer)
        )
        q_copies[i].start()
    q_all[z] = q_pack[z]

    for i in range(1, PLANE):
        kv_copies[i - 1].wait_recv()
        down_column(i)
        if i > LAG:
            across_column(i - LAG - 1)

    for i in range(3):
        og_copies[i].wait_recv()
        slot = 2 * lax.rem(x + 3 - i, 4) + core
        copy = remote(og_all.at[slot], og_all.at[slot], oc_s.at[i], oc_r.at[i], dp=partner)
        copy.start()
        og_core.append(copy)
    for i in range(PLANE - LAG - 1, PLANE):
        across_column(i)
    for copy in wy_copies:
        copy.wait()
    for copy in og_core:
        copy.wait_recv()

    weight = w_all[...].reshape(CTX, 1, 16, 128)
    none = jnp.zeros_like(weight)
    low4 = lax.broadcasted_iota(jnp.int32, weight.shape, 3) < HEAD_DIM
    weight = jnp.concatenate(
        [jnp.where(low4, weight, none), jnp.where(low4, none, weight)], axis=1
    ).reshape(CTX * 32, 128)
    for s in range(PLANE):
        grad = dot(og_all[s], weight)
        grad = grad + pltpu.roll(grad, HEAD_DIM, 1)
        g_pack[s] = jnp.where(low, grad[:BLK], grad[BLK:]).astype(BF16)
    g_copies = []
    head = lax.rem(part + z, HEADS)
    for i in range(PLANE):
        peer = lax.rem(part + i, PLANE)
        copy = remote(g_pack.at[peer], g_all.at[z], g_s.at[i], g_r.at[z],
                      dp=base + peer, ctx=col * PLANE + head)
        g_copies.append(copy)
        if i:
            copy.start()
        else:
            pl.when(jnp.logical_not(stays))(copy.start)

            @pl.when(stays)
            def _():
                g_all[z] = g_pack[part]

    for s in range(PLANE):
        og_t[:, 128 * s:128 * s + 128] = og_all[s].T
    for i in range(PLANE):
        (to_left if i % 2 == 0 else to_right)[i].wait_recv()
    for copy in q_copies + far:
        copy.wait_recv()

    length = tab[T_LENGTH]
    lane = lax.broadcasted_iota(jnp.int32, (1, 128), 1)
    row = lax.broadcasted_iota(jnp.int32, (BLK, 1), 0)
    entry = lax.broadcasted_iota(jnp.int32, (1, KPQ * BLK), 1) // BLK

    def listed(u):
        blocks = [tab[T_LIST + u * KPQ + j] for j in range(KPQ)]
        return blocks, jnp.concatenate([kv_all[b] for b in blocks], axis=0)

    def forward(zp, carry):
        query = q_all[zp].astype(F32) * FACTOR
        outs = []
        for p in range(2):
            u = 2 * zp + p
            blocks, keyval = listed(u)
            left = query if p == 0 else pltpu.roll(query, HEAD_DIM, 1)
            scores = dot(jnp.where(low, left, 0.0).astype(BF16), keyval, ((1,), (1,)))
            place = jnp.concatenate(
                [
                    jnp.where(lane < BLK, blocks[j] * BLK + lane, blocks[j + 1] * BLK + lane - BLK)
                    for j in range(0, KPQ, 2)
                ],
                axis=1,
            )
            own = (col * UNITS + u) * BLK + row
            allowed = (entry < tab[T_COUNT + u]) & ((place < length) | (place == own))
            scores = jnp.where(allowed, scores, -jnp.inf)
            exponent = jnp.exp(scores - jnp.max(scores, axis=1, keepdims=True))
            probs = exponent * (1.0 / jnp.sum(exponent, axis=1, keepdims=True))
            probs = probs.astype(BF16)
            p_all[u] = probs
            outs.append(dot(probs, keyval) * (own < length).astype(F32))
        o_pack[zp] = pair_up(outs[0], outs[1], 1).astype(BF16)
        return carry

    lax.fori_loop(0, PLANE, forward, 0, unroll=2)

    o_copies = []
    for i in range(PLANE):
        peer = lax.rem(z + i, PLANE)
        copy = remote(o_pack.at[peer], o_all.at[part], o_s.at[i], o_r.at[part],
                      dp=base + z, ctx=col * PLANE + peer)
        o_copies.append(copy)
        if i:
            copy.start()
        else:
            pl.when(jnp.logical_not(here))(copy.start)

            @pl.when(here)
            def _():
                o_all[part] = o_pack[z]

    def arrived(dst, sem):
        remote(dst, dst, sem, sem, dp=dp, ctx=me).wait_recv()

    for i in range(1, PLANE):
        slot = lax.rem(z + i, PLANE)
        arrived(g_all.at[slot], g_r.at[slot])

    @pl.when(jnp.logical_not(stays))
    def _():
        arrived(g_all.at[z], g_r.at[z])

    def backward(zp, carry):
        query = q_all[zp].astype(F32) * FACTOR
        grads = g_all[zp].astype(F32)
        outs = []
        for p in range(2):
            u = 2 * zp + p
            _, keyval = listed(u)
            valid = ((col * UNITS + u) * BLK + row < length).astype(F32)
            if p == 0:
                top, bottom = query, pltpu.roll(grads, HEAD_DIM, 1)
            else:
                top, bottom = pltpu.roll(query, HEAD_DIM, 1), grads
            top = jnp.where(low, top, 0.0).astype(BF16)
            bottom = jnp.where(low, 0.0, bottom * valid).astype(BF16)
            prob_grad = dot(bottom, keyval, ((1,), (1,)))
            probs16 = p_all[u]
            probs = probs16.astype(F32)
            delta = jnp.sum(probs * prob_grad, axis=1, keepdims=True)
            score_grad = (probs * (prob_grad - delta)).astype(BF16)
            outs.append(dot(score_grad, keyval) * FACTOR)
            stacked = jnp.concatenate([score_grad, probs16], axis=0)
            grad = dot(stacked, jnp.concatenate([top, bottom], axis=0), ((0,), (0,)))
            for j in range(KPQ):
                entry_grads[u * KPQ + j] = grad[j * BLK:(j + 1) * BLK]
        dq_pack[zp] = pair_up(outs[0], outs[1], 0).astype(BF16)
        return carry

    lax.fori_loop(0, PLANE, backward, 0, unroll=2)

    dq_copies = []
    for i, peer in enumerate(z_peers):
        copy = remote(dq_pack.at[peer], dq_all.at[z], dq_s.at[i], dq_r.at[i], ctx=col * PLANE + peer)
        copy.start()
        dq_copies.append(copy)
    dq_all[z] = dq_pack[z]

    sums[ENTRIES] = jnp.zeros((BLK, 128), F32)

    def accumulate(t, total):
        total = entry_grads[tab[T_PERM + t]] + total * tab[T_SAME + t].astype(F32)
        sums[t] = total
        return total

    lax.fori_loop(0, ENTRIES, accumulate, jnp.zeros((BLK, 128), F32), unroll=4)

    def pack(c, carry):
        for half in range(2):
            dkv_pack[c, half] = sums[tab[T_LAST + 2 * c + half]].astype(BF16)
        return carry

    lax.fori_loop(0, CTX, pack, 0, unroll=2)
    dkvy_copies, dkv_copies = [], []

    def send_dkv(i):
        zc = lax.rem(z + 1 + i, PLANE)
        for j, peer in enumerate(col_peers):
            copy = remote(dkv_pack.at[peer * PLANE + zc], dkv_y.at[j, zc], dkvy_s.at[3 * i + j],
                          dkvy_r.at[3 * i + j], ctx=peer * PLANE + z)
            copy.start()
            dkvy_copies.append(copy)

    for i in range(2):
        send_dkv(i)

    for i in range(1, PLANE):
        slot = lax.rem(part + i, PLANE)
        arrived(o_all.at[slot], o_r.at[slot])

    @pl.when(jnp.logical_not(here))
    def _():
        arrived(o_all.at[part], o_r.at[part])

    attention = o_all[...].reshape(PLANE, 1, BLK, 128)
    none = jnp.zeros_like(attention)
    low4 = lax.broadcasted_iota(jnp.int32, attention.shape, 3) < HEAD_DIM
    attention = jnp.concatenate(
        [jnp.where(low4, attention, none), jnp.where(low4, none, attention)], axis=1
    ).reshape(PLANE * 128, 128)
    for c in range(0, CTX, 8):
        grad = dot(og_t[32 * c:32 * c + 256], attention)
        grad = ((grad + pltpu.roll(grad, HEAD_DIM, 1)) * WG_SCALE).reshape(8, 2, 16, 128)
        for k in range(8):
            wg_pack[c // PLANE, k] = jnp.where(low16, grad[k, 0], grad[k, 1]).astype(BF16)
    by_copies, b_copies, c_copies = [], [], []
    for j, peer in enumerate(col_peers):
        copy = remote(wg_pack.at[peer], wg_in.at[col], by_s.at[j], by_r.at[j], ctx=peer * PLANE + z)
        copy.start()
        by_copies.append(copy)
    wg_in[col] = wg_pack[col]

    for i in range(2, PLANE):
        send_dkv(i)

    for copy in by_copies:
        copy.wait()
    wg_mid[...] = sum(wg_in[i].astype(F32) for i in range(COLS)).astype(BF16)
    for i, peer in enumerate(z_peers):
        copy = remote(wg_mid.at[peer], wg_col.at[z], b_s.at[i], b_r.at[i], ctx=col * PLANE + peer)
        copy.start()
        b_copies.append(copy)
    wg_col[z] = wg_mid[z]

    for i in range(PLANE):
        zc = lax.rem(z + 1 + i, PLANE)
        for j in range(COLS - 1):
            dkvy_copies[3 * i + j].wait_recv()
        total = dkv_pack[col * PLANE + zc].astype(F32)
        for j in range(COLS - 1):
            total = total + dkv_y[j, zc].astype(F32)
        if i == PLANE - 1:
            dkv_in[z] = total.astype(BF16)
        else:
            dkv_z[i] = total.astype(BF16)
            copy = remote(dkv_z.at[i], dkv_in.at[z], dkv_s.at[i], dkv_r.at[i], ctx=col * PLANE + zc)
            copy.start()
            dkv_copies.append(copy)
        if i == 1:
            for copy in b_copies:
                copy.wait()
            wg_last[...] = sum(wg_col[k].astype(F32) for k in range(PLANE)).astype(BF16)
            for k, peer in enumerate(dp_peers):
                copy = remote(wg_last, wg_all.at[dp], c_s.at[k], c_r.at[k], dp=peer)
                copy.start()
                c_copies.append(copy)
            wg_all[dp] = wg_last[...]

    for copy in dq_copies:
        copy.wait()
    for c in range(4):
        for half in range(2):
            dq_out[BLK * half:BLK * half + BLK, 128 * c:128 * c + 128] = pair_up(
                dq_all[2 * c], dq_all[2 * c + 1], half
            ).astype(BF16)

    for copy in c_copies:
        copy.wait()
    for c in range(4):
        even = wg_all[2 * c].astype(F32) + wg_all[PLANE + 2 * c].astype(F32)
        odd_ = wg_all[2 * c + 1].astype(F32) + wg_all[PLANE + 2 * c + 1].astype(F32)
        for half in range(2):
            wg_out[16 * half:16 * half + 16, 128 * c:128 * c + 128] = pair_up(even, odd_, half)

    for copy in dkv_copies:
        copy.wait()
    for c in range(4):
        for half in range(2):
            rows = slice(BLK * half, BLK * half + BLK)
            even, odd_ = dkv_in[2 * c, half], dkv_in[2 * c + 1, half]
            dkv_out[rows, 128 * c:128 * c + 128] = pair_up(even, odd_, 0).astype(BF16)
            dkv_out[rows, 512 + 128 * c:640 + 128 * c] = pair_up(even, odd_, 1).astype(BF16)

    for copy in (og_copies + og_core + q_copies + kv_copies + kvy_copies + dkvy_copies
                 + g_copies[1:] + o_copies[1:]):
        copy.wait_send()

    @pl.when(jnp.logical_not(here))
    def _():
        o_copies[0].wait_send()

    @pl.when(jnp.logical_not(stays))
    def _():
        g_copies[0].wait_send()


def table(block_list, counts, length, first):
    mine = lax.dynamic_slice_in_dim(block_list, first, UNITS, 0).reshape(ENTRIES)
    ids = jnp.arange(ENTRIES, dtype=jnp.int32)
    key = mine * ENTRIES + ids
    place = jnp.sum((key[None, :] < key[:, None]).astype(jnp.int32), axis=1)
    at = place[None, :] == ids[:, None]
    perm = jnp.sum(jnp.where(at, ids[None, :], 0), axis=1)
    same = (mine[None, :] == mine[:, None]) & (ids[None, :] < ids[:, None])
    later = jnp.max(same.astype(jnp.int32), axis=1)
    go_on = jnp.sum(jnp.where(at, later[None, :], 0), axis=1)
    blocks = jnp.arange(NQB, dtype=jnp.int32)
    upto = jnp.sum((mine[None, :] <= blocks[:, None]).astype(jnp.int32), axis=1)
    named = jnp.max((mine[None, :] == blocks[:, None]).astype(jnp.int32), axis=1)
    last = jnp.where(named > 0, upto - 1, ENTRIES)
    mine_counts = lax.dynamic_slice_in_dim(counts, first, UNITS, 0)
    return jnp.concatenate([mine, perm, go_on, last, mine_counts, length])


def per_device(queries, keyvals, out_weight, out_grad, block_lists, block_counts, seq_lengths):
    first = (lax.axis_index("ctx") // PLANE) * UNITS
    tab = table(block_lists[0], block_counts[0], seq_lengths, first)
    dma = pltpu.SemaphoreType.DMA
    vm = pltpu.VMEM
    hbm = pl.BlockSpec(memory_space=pltpu.HBM)
    zs, ys = PLANE - 1, COLS - 1
    pairs = [zs, ys, 3, 4, zs, zs, PLANE * ys, PLANE, PLANE, zs, PLANE * ys, zs, zs, ys, DP - 1]
    return pl.pallas_call(
        body,
        out_shape=(
            jax.ShapeDtypeStruct((128, 512), BF16),
            jax.ShapeDtypeStruct((128, 1024), BF16),
            jax.ShapeDtypeStruct((32, 512), F32),
        ),
        in_specs=[pl.BlockSpec(memory_space=pltpu.SMEM)] + [hbm] * 4,
        out_specs=tuple([pl.BlockSpec(memory_space=pltpu.VMEM)] * 3),
        scratch_shapes=[
            vm((128, 512), BF16), vm((128, 1024), BF16), vm((32, 512), BF16),
            vm((HEADS, 16, 128), BF16), vm((CTX, 16, 128), BF16),
            vm((PLANE, 128, 1024), BF16), vm((1024, 1024), BF16),
            vm((HEADS, BLK, 128), BF16), vm((PLANE, BLK, 128), BF16),
            vm((HEADS, 2, BLK, 128), BF16), vm((NQB, BLK, 128), BF16),
            vm((PLANE, BLK, 128), BF16), vm((PLANE, BLK, 128), BF16),
            vm((UNITS, BLK, KPQ * BLK), BF16),
            vm((PLANE, BLK, 128), BF16), vm((PLANE, BLK, 128), BF16),
            vm((PLANE, BLK, 128), BF16), vm((PLANE, BLK, 128), BF16),
            vm((ENTRIES, BLK, 128), F32), vm((ENTRIES + 1, BLK, 128), F32),
            vm((CTX, 2, BLK, 128), BF16), vm((COLS - 1, PLANE, 2, BLK, 128), BF16),
            vm((PLANE - 1, 2, BLK, 128), BF16), vm((HEADS, 2, BLK, 128), BF16),
            vm((COLS, PLANE, 16, 128), BF16), vm((COLS, PLANE, 16, 128), BF16),
            vm((PLANE, 16, 128), BF16), vm((PLANE, 16, 128), BF16),
            vm((16, 128), BF16), vm((DP, 16, 128), BF16),
            dma((4,)),
        ] + [dma((n,)) for n in pairs for _ in range(2)],
        compiler_params=pltpu.CompilerParams(
            collective_id=0, has_side_effects=True, vmem_limit_bytes=60 * 2**20
        ),
        name="attention_step",
    )(tab, queries, keyvals, out_weight, out_grad)


def solution(mesh):
    placed = (
        P(("dp", "ctx"), None),
        P(("dp", "ctx"), None),
        P("ctx", None),
        P(("dp", "ctx"), None),
        P("dp", None, None),
        P("dp", None),
        P("dp"),
    )
    return jax.shard_map(
        per_device,
        mesh=mesh,
        in_specs=placed,
        out_specs=(P(("dp", "ctx"), None), P(("dp", "ctx"), None), P("ctx", None)),
        check_vma=False,
    )
```

```python
import math

import jax
import jax.numpy as jnp
from jax import lax
from jax.experimental import pallas as pl
from jax.experimental.pallas import tpu as pltpu
from jax.sharding import PartitionSpec as P

HEADS = 8
HEAD_DIM = 64
BLK = 64
KPQ = 8
NQB = 64
CTX = 32
COLS = 4
LAG = 2
DP = 16
PLANE = 8
UNITS = 16
ENTRIES = UNITS * KPQ
FACTOR = 1.0 / math.sqrt(HEAD_DIM)
WG_SCALE = 1.0 / math.sqrt(128 * CTX * DP)
MESH = pl.DeviceIdType.MESH
BF16 = jnp.bfloat16
F32 = jnp.float32

T_LIST = 0
T_PERM = T_LIST + ENTRIES
T_SAME = T_PERM + ENTRIES
T_LAST = T_SAME + ENTRIES
T_COUNT = T_LAST + NQB
T_LENGTH = T_COUNT + UNITS


def low_half(shape):
    return lax.broadcasted_iota(jnp.int32, shape, 1) < HEAD_DIM


def pair_up(first, second, which):
    first, second = first.astype(F32), second.astype(F32)
    low = low_half(first.shape)
    if which == 0:
        return jnp.where(low, first, pltpu.roll(second, HEAD_DIM, 1))
    return jnp.where(low, pltpu.roll(first, HEAD_DIM, 1), second)


def dot(a, b, dims=((1,), (0,))):
    return lax.dot_general(a, b, (dims, ((), ())), preferred_element_type=F32)


def remote(src, dst, send, recv, **where):
    return pltpu.make_async_remote_copy(
        src_ref=src, dst_ref=dst, send_sem=send, recv_sem=recv,
        device_id=where, device_id_type=MESH,
    )


def body(tab, q_hbm, kv_hbm, w_hbm, og_hbm, dq_out, dkv_out, wg_out,
         q_ref, kv_ref, w_ref, w_tile, w_all, og_all, og_t, q_pack, q_all, kv_pack, kv_all,
         g_pack, g_all, p_all, o_pack, o_all, dq_pack, dq_all, entry_grads, sums,
         dkv_pack, dkv_y, dkv_mix, dkv_z, dkv_in, wg_pack, wg_in, wg_mid, wg_col, wg_last, wg_all,
         in_sem, w_s, w_r, wy_s, wy_r, og_s, og_r, oc_s, oc_r, q_s, q_r, kv_s, kv_r, kvy_s, kvy_r,
         g_s, g_r, o_s, o_r, dq_s, dq_r, dkvy_s, dkvy_r, dkv_s, dkv_r, b_s, b_r, by_s, by_r,
         c_s, c_r):
    dp = lax.axis_index("dp")
    me = lax.axis_index("ctx")
    col, z = me // PLANE, lax.rem(me, PLANE)
    part = lax.rem(dp, PLANE)
    base = dp - part
    x, core = part // 2, lax.rem(part, 2)
    partner = base + 2 * x + 1 - core
    col_peers = [lax.rem(col + i, COLS) for i in range(1, COLS)]
    dp_peers = [lax.rem(dp + i, DP) for i in range(1, DP)]
    z_peers = [lax.rem(z + i, PLANE) for i in range(1, PLANE)]
    x_peers = [lax.rem(x + i, 4) for i in range(1, 4)]
    here = part == z

    loads = [
        pltpu.make_async_copy(w_hbm, w_ref, in_sem.at[0]),
        pltpu.make_async_copy(og_hbm, og_all.at[part], in_sem.at[1]),
        pltpu.make_async_copy(q_hbm, q_ref, in_sem.at[2]),
        pltpu.make_async_copy(kv_hbm, kv_ref, in_sem.at[3]),
    ]
    for copy in loads:
        copy.start()

    barrier = pltpu.get_barrier_semaphore()

    def greet(**where):
        pl.semaphore_signal(barrier, inc=1, device_id=where, device_id_type=MESH)

    for peer in z_peers:
        greet(ctx=col * PLANE + peer)
    for peer in col_peers:
        greet(ctx=peer * PLANE + z)
    for peer in dp_peers:
        greet(dp=peer)
    for i in range(1, PLANE):
        other = lax.rem(part + i, PLANE)
        greet(dp=base + other, ctx=col * PLANE + part)
        greet(dp=base + other, ctx=col * PLANE + lax.rem(z + PLANE - other, PLANE))
    stays = part == 0

    @pl.when(jnp.logical_not(here))
    def _():
        greet(dp=dp, ctx=col * PLANE + part)

    @pl.when(jnp.logical_not(stays))
    def _():
        greet(dp=dp, ctx=col * PLANE + lax.rem(z + PLANE - part, PLANE))

    low16 = low_half((16, 128))
    low = low_half((BLK, 128))
    loads[0].wait()
    for head in range(HEADS):
        cols = slice(128 * (head // 2), 128 * (head // 2) + 128)
        w_tile[head] = pair_up(w_ref[:16, cols], w_ref[16:, cols], head % 2).astype(BF16)
    w_all[me] = w_tile[lax.rem(part + z, HEADS)]
    loads[2].wait()
    for head in range(HEADS):
        cols = slice(128 * (head // 2), 128 * (head // 2) + 128)
        q_pack[head] = pair_up(q_ref[:BLK, cols], q_ref[BLK:, cols], head % 2).astype(BF16)
    loads[3].wait()
    for head in range(HEADS):
        first = 128 * (head // 2)
        for half in range(2):
            rows = slice(BLK * half, BLK * half + BLK)
            kv_pack[head, half] = pair_up(
                kv_ref[rows, first:first + 128], kv_ref[rows, 512 + first:640 + first], head % 2
            ).astype(BF16)
    loads[1].wait()

    barrier_count = PLANE - 1 + COLS - 1 + DP - 1 + 2 * (PLANE - 1)
    barrier_count = barrier_count + jnp.where(here, 0, 1) + jnp.where(stays, 0, 1)
    pl.semaphore_wait(barrier, barrier_count)

    w_copies, wy_copies, og_copies, og_core, q_copies, kv_copies, kvy_copies = [], [], [], [], [], [], []

    def rank_rows(ref, rank):
        return ref.at[pl.ds(2 * rank, 2)]

    right, left = lax.rem(col + 1, COLS), lax.rem(col + COLS - 1, COLS)
    to_right, to_left = [], []

    def pass_on(rank, n, to, kept):
        rows = rank_rows(kv_all, rank)
        copy = remote(rows, rows, kvy_s.at[n], kvy_r.at[n], ctx=to * PLANE + z)
        copy.start()
        kept.append(copy)
        kvy_copies.append(copy)

    def down_column(i):
        rank = col * PLANE + lax.rem(z + PLANE - i, PLANE)
        pass_on(rank, 2 * i, right, to_right)
        pass_on(rank, 2 * i + 1, left, to_left)

    def across_column(i):
        at = lax.rem(z + PLANE - i, PLANE)
        if i % 2 == 0:
            to_right[i].wait_recv()
            pass_on(left * PLANE + at, 2 * PLANE + i, right, far)
        else:
            to_left[i].wait_recv()
            pass_on(right * PLANE + at, 2 * PLANE + i, left, far)

    far = []
    for i, peer in enumerate(z_peers):
        w_copies.append(
            remote(w_tile.at[lax.rem(part + peer, HEADS)], w_all.at[me], w_s.at[i], w_r.at[i],
                   ctx=col * PLANE + peer)
        )
        w_copies[i].start()
    mine = og_all.at[part]
    for i, peer in enumerate(x_peers):
        og_copies.append(remote(mine, mine, og_s.at[i], og_r.at[i], dp=base + 2 * peer + core))
        og_copies[i].start()
    for i, peer in enumerate(z_peers):
        copy = remote(kv_pack.at[peer], rank_rows(kv_all, me), kv_s.at[i], kv_r.at[i],
                      ctx=col * PLANE + peer)
        copy.start()
        kv_copies.append(copy)
    kv_all[pl.ds(2 * me, 2)] = kv_pack[z]
    down_column(0)
    og_core.append(remote(mine, mine, oc_s.at[3], oc_r.at[3], dp=partner))
    og_core[0].start()
    for copy in w_copies:
        copy.wait()
    for j, peer in enumerate(col_peers):
        rows = w_all.at[pl.ds(col * PLANE, PLANE)]
        copy = remote(rows, rows, wy_s.at[j], wy_r.at[j], ctx=peer * PLANE + z)
        copy.start()
        wy_copies.append(copy)
    for i, peer in enumerate(z_peers):
        q_copies.append(
            remote(q_pack.at[peer], q_all.at[z], q_s.at[i], q_r.at[i], ctx=col * PLANE + peer)
        )
        q_copies[i].start()
    q_all[z] = q_pack[z]

    for i in range(1, PLANE):
        kv_copies[i - 1].wait_recv()
        down_column(i)
        if i > LAG:
            across_column(i - LAG - 1)

    for i in range(3):
        og_copies[i].wait_recv()
        slot = 2 * lax.rem(x + 3 - i, 4) + core
        copy = remote(og_all.at[slot], og_all.at[slot], oc_s.at[i], oc_r.at[i], dp=partner)
        copy.start()
        og_core.append(copy)
    for copy in wy_copies:
        copy.wait()
    for copy in og_core:
        copy.wait_recv()

    weight = w_all[...].reshape(CTX, 1, 16, 128)
    none = jnp.zeros_like(weight)
    low4 = lax.broadcasted_iota(jnp.int32, weight.shape, 3) < HEAD_DIM
    weight = jnp.concatenate(
        [jnp.where(low4, weight, none), jnp.where(low4, none, weight)], axis=1
    ).reshape(CTX * 32, 128)
    for s in range(PLANE):
        grad = dot(og_all[s], weight)
        grad = grad + pltpu.roll(grad, HEAD_DIM, 1)
        g_pack[s] = jnp.where(low, grad[:BLK], grad[BLK:]).astype(BF16)
    g_copies = []
    head = lax.rem(part + z, HEADS)
    for i in range(PLANE):
        peer = lax.rem(part + i, PLANE)
        copy = remote(g_pack.at[peer], g_all.at[z], g_s.at[i], g_r.at[z],
                      dp=base + peer, ctx=col * PLANE + head)
        g_copies.append(copy)
        if i:
            copy.start()
        else:
            pl.when(jnp.logical_not(stays))(copy.start)

            @pl.when(stays)
            def _():
                g_all[z] = g_pack[part]

    for i in range(PLANE - LAG - 1, PLANE):
        across_column(i)
    for s in range(PLANE):
        og_t[:, 128 * s:128 * s + 128] = og_all[s].T
    for i in range(PLANE):
        (to_left if i % 2 == 0 else to_right)[i].wait_recv()
    for copy in q_copies + far:
        copy.wait_recv()

    length = tab[T_LENGTH]
    lane = lax.broadcasted_iota(jnp.int32, (1, 128), 1)
    row = lax.broadcasted_iota(jnp.int32, (BLK, 1), 0)
    entry = lax.broadcasted_iota(jnp.int32, (1, KPQ * BLK), 1) // BLK

    def listed(u):
        blocks = [tab[T_LIST + u * KPQ + j] for j in range(KPQ)]
        return blocks, jnp.concatenate([kv_all[b] for b in blocks], axis=0)

    def forward(zp, carry):
        query = q_all[zp].astype(F32) * FACTOR
        outs = []
        for p in range(2):
            u = 2 * zp + p
            blocks, keyval = listed(u)
            left = query if p == 0 else pltpu.roll(query, HEAD_DIM, 1)
            scores = dot(jnp.where(low, left, 0.0).astype(BF16), keyval, ((1,), (1,)))
            place = jnp.concatenate(
                [
                    jnp.where(lane < BLK, blocks[j] * BLK + lane, blocks[j + 1] * BLK + lane - BLK)
                    for j in range(0, KPQ, 2)
                ],
                axis=1,
            )
            own = (col * UNITS + u) * BLK + row
            allowed = (entry < tab[T_COUNT + u]) & ((place < length) | (place == own))
            scores = jnp.where(allowed, scores, -jnp.inf)
            exponent = jnp.exp(scores - jnp.max(scores, axis=1, keepdims=True))
            probs = exponent * (1.0 / jnp.sum(exponent, axis=1, keepdims=True))
            probs = probs.astype(BF16)
            p_all[u] = probs
            outs.append(dot(probs, keyval) * (own < length).astype(F32))
        o_pack[zp] = pair_up(outs[0], outs[1], 1).astype(BF16)
        return carry

    lax.fori_loop(0, PLANE, forward, 0, unroll=2)

    o_copies = []
    for i in range(PLANE):
        peer = lax.rem(z + i, PLANE)
        copy = remote(o_pack.at[peer], o_all.at[part], o_s.at[i], o_r.at[part],
                      dp=base + z, ctx=col * PLANE + peer)
        o_copies.append(copy)
        if i:
            copy.start()
        else:
            pl.when(jnp.logical_not(here))(copy.start)

            @pl.when(here)
            def _():
                o_all[part] = o_pack[z]

    def arrived(dst, sem):
        remote(dst, dst, sem, sem, dp=dp, ctx=me).wait_recv()

    for i in range(1, PLANE):
        slot = lax.rem(z + i, PLANE)
        arrived(g_all.at[slot], g_r.at[slot])

    @pl.when(jnp.logical_not(stays))
    def _():
        arrived(g_all.at[z], g_r.at[z])

    def backward(zp, carry):
        query = q_all[zp].astype(F32) * FACTOR
        grads = g_all[zp].astype(F32)
        outs = []
        for p in range(2):
            u = 2 * zp + p
            _, keyval = listed(u)
            valid = ((col * UNITS + u) * BLK + row < length).astype(F32)
            if p == 0:
                top, bottom = query, pltpu.roll(grads, HEAD_DIM, 1)
            else:
                top, bottom = pltpu.roll(query, HEAD_DIM, 1), grads
            top = jnp.where(low, top, 0.0).astype(BF16)
            bottom = jnp.where(low, 0.0, bottom * valid).astype(BF16)
            prob_grad = dot(bottom, keyval, ((1,), (1,)))
            probs16 = p_all[u]
            probs = probs16.astype(F32)
            delta = jnp.sum(probs * prob_grad, axis=1, keepdims=True)
            score_grad = (probs * (prob_grad - delta)).astype(BF16)
            outs.append(dot(score_grad, keyval) * FACTOR)
            stacked = jnp.concatenate([score_grad, probs16], axis=0)
            grad = dot(stacked, jnp.concatenate([top, bottom], axis=0), ((0,), (0,)))
            for j in range(KPQ):
                entry_grads[u * KPQ + j] = grad[j * BLK:(j + 1) * BLK]
        dq_pack[zp] = pair_up(outs[0], outs[1], 0).astype(BF16)
        return carry

    lax.fori_loop(0, PLANE, backward, 0, unroll=2)

    dq_copies = []
    for i, peer in enumerate(z_peers):
        copy = remote(dq_pack.at[peer], dq_all.at[z], dq_s.at[i], dq_r.at[i], ctx=col * PLANE + peer)
        copy.start()
        dq_copies.append(copy)
    dq_all[z] = dq_pack[z]

    sums[ENTRIES] = jnp.zeros((BLK, 128), F32)

    def accumulate(t, total):
        total = entry_grads[tab[T_PERM + t]] + total * tab[T_SAME + t].astype(F32)
        sums[t] = total
        return total

    lax.fori_loop(0, ENTRIES, accumulate, jnp.zeros((BLK, 128), F32), unroll=4)

    def pack(c, carry):
        for half in range(2):
            dkv_pack[c, half] = sums[tab[T_LAST + 2 * c + half]].astype(BF16)
        return carry

    lax.fori_loop(0, CTX, pack, 0, unroll=2)
    dkvy_copies, dkv_copies = [], []

    opposite = lax.rem(col + 2, COLS)
    far_copies, mixed_copies = [], []

    def step_dkv(i, n, src, slot, to):
        zc = lax.rem(z + 1 + i, PLANE)
        copy = remote(src, dkv_y.at[slot, zc], dkvy_s.at[3 * i + n], dkvy_r.at[3 * i + n],
                      ctx=to * PLANE + z)
        copy.start()
        return copy

    def send_dkv(i):
        zc = lax.rem(z + 1 + i, PLANE)
        ahead, behind = (right, left) if i % 2 == 0 else (left, right)
        far_copies.append(step_dkv(i, 0, dkv_pack.at[opposite * PLANE + zc], 2, ahead))
        dkvy_copies.append(step_dkv(i, 1, dkv_pack.at[behind * PLANE + zc], 0, behind))

    def mix_dkv(i):
        zc = lax.rem(z + 1 + i, PLANE)
        ahead = right if i % 2 == 0 else left
        far_copies[i].wait_recv()
        total = dkv_pack[ahead * PLANE + zc].astype(F32) + dkv_y[2, zc].astype(F32)
        dkv_mix[i] = total.astype(BF16)
        mixed_copies.append(step_dkv(i, 2, dkv_mix.at[i], 1, ahead))

    for i in range(2):
        send_dkv(i)

    for i in range(1, PLANE):
        slot = lax.rem(part + i, PLANE)
        arrived(o_all.at[slot], o_r.at[slot])

    @pl.when(jnp.logical_not(here))
    def _():
        arrived(o_all.at[part], o_r.at[part])

    attention = o_all[...].reshape(PLANE, 1, BLK, 128)
    none = jnp.zeros_like(attention)
    low4 = lax.broadcasted_iota(jnp.int32, attention.shape, 3) < HEAD_DIM
    attention = jnp.concatenate(
        [jnp.where(low4, attention, none), jnp.where(low4, none, attention)], axis=1
    ).reshape(PLANE * 128, 128)
    for c in range(0, CTX, 8):
        grad = dot(og_t[32 * c:32 * c + 256], attention)
        grad = ((grad + pltpu.roll(grad, HEAD_DIM, 1)) * WG_SCALE).reshape(8, 2, 16, 128)
        for k in range(8):
            wg_pack[c // PLANE, k] = jnp.where(low16, grad[k, 0], grad[k, 1]).astype(BF16)
    by_copies, b_copies, c_copies = [], [], []
    for j, peer in enumerate(col_peers):
        copy = remote(wg_pack.at[peer], wg_in.at[col], by_s.at[j], by_r.at[j], ctx=peer * PLANE + z)
        copy.start()
        by_copies.append(copy)
    wg_in[col] = wg_pack[col]

    for i in range(2, PLANE):
        send_dkv(i)
        mix_dkv(i - 2)

    for copy in by_copies:
        copy.wait()
    wg_mid[...] = sum(wg_in[i].astype(F32) for i in range(COLS)).astype(BF16)
    for i, peer in enumerate(z_peers):
        copy = remote(wg_mid.at[peer], wg_col.at[z], b_s.at[i], b_r.at[i], ctx=col * PLANE + peer)
        copy.start()
        b_copies.append(copy)
    wg_col[z] = wg_mid[z]

    for i in range(PLANE):
        zc = lax.rem(z + 1 + i, PLANE)
        if i < 2:
            mix_dkv(PLANE - 2 + i)
        dkvy_copies[i].wait_recv()
        mixed_copies[i].wait_recv()
        total = dkv_pack[col * PLANE + zc].astype(F32)
        for j in range(2):
            total = total + dkv_y[j, zc].astype(F32)
        if i == PLANE - 1:
            dkv_in[z] = total.astype(BF16)
        else:
            dkv_z[i] = total.astype(BF16)
            copy = remote(dkv_z.at[i], dkv_in.at[z], dkv_s.at[i], dkv_r.at[i], ctx=col * PLANE + zc)
            copy.start()
            dkv_copies.append(copy)
        if i == 1:
            for copy in b_copies:
                copy.wait()
            wg_last[...] = sum(wg_col[k].astype(F32) for k in range(PLANE)).astype(BF16)
            for k, peer in enumerate(dp_peers):
                copy = remote(wg_last, wg_all.at[dp], c_s.at[k], c_r.at[k], dp=peer)
                copy.start()
                c_copies.append(copy)
            wg_all[dp] = wg_last[...]

    for copy in dq_copies:
        copy.wait()
    for c in range(4):
        for half in range(2):
            dq_out[BLK * half:BLK * half + BLK, 128 * c:128 * c + 128] = pair_up(
                dq_all[2 * c], dq_all[2 * c + 1], half
            ).astype(BF16)

    for copy in c_copies:
        copy.wait()
    for c in range(4):
        even = wg_all[2 * c].astype(F32) + wg_all[PLANE + 2 * c].astype(F32)
        odd_ = wg_all[2 * c + 1].astype(F32) + wg_all[PLANE + 2 * c + 1].astype(F32)
        for half in range(2):
            wg_out[16 * half:16 * half + 16, 128 * c:128 * c + 128] = pair_up(even, odd_, half)

    for copy in dkv_copies:
        copy.wait()
    for c in range(4):
        for half in range(2):
            rows = slice(BLK * half, BLK * half + BLK)
            even, odd_ = dkv_in[2 * c, half], dkv_in[2 * c + 1, half]
            dkv_out[rows, 128 * c:128 * c + 128] = pair_up(even, odd_, 0).astype(BF16)
            dkv_out[rows, 512 + 128 * c:640 + 128 * c] = pair_up(even, odd_, 1).astype(BF16)

    for copy in (og_copies + og_core + q_copies + kv_copies + kvy_copies + dkvy_copies + far_copies
                 + mixed_copies + g_copies[1:] + o_copies[1:]):
        copy.wait_send()

    @pl.when(jnp.logical_not(here))
    def _():
        o_copies[0].wait_send()

    @pl.when(jnp.logical_not(stays))
    def _():
        g_copies[0].wait_send()


def table(block_list, counts, length, first):
    mine = lax.dynamic_slice_in_dim(block_list, first, UNITS, 0).reshape(ENTRIES)
    ids = jnp.arange(ENTRIES, dtype=jnp.int32)
    key = mine * ENTRIES + ids
    place = jnp.sum((key[None, :] < key[:, None]).astype(jnp.int32), axis=1)
    at = place[None, :] == ids[:, None]
    perm = jnp.sum(jnp.where(at, ids[None, :], 0), axis=1)
    same = (mine[None, :] == mine[:, None]) & (ids[None, :] < ids[:, None])
    later = jnp.max(same.astype(jnp.int32), axis=1)
    go_on = jnp.sum(jnp.where(at, later[None, :], 0), axis=1)
    blocks = jnp.arange(NQB, dtype=jnp.int32)
    upto = jnp.sum((mine[None, :] <= blocks[:, None]).astype(jnp.int32), axis=1)
    named = jnp.max((mine[None, :] == blocks[:, None]).astype(jnp.int32), axis=1)
    last = jnp.where(named > 0, upto - 1, ENTRIES)
    mine_counts = lax.dynamic_slice_in_dim(counts, first, UNITS, 0)
    return jnp.concatenate([mine, perm, go_on, last, mine_counts, length])


def per_device(queries, keyvals, out_weight, out_grad, block_lists, block_counts, seq_lengths):
    first = (lax.axis_index("ctx") // PLANE) * UNITS
    tab = table(block_lists[0], block_counts[0], seq_lengths, first)
    dma = pltpu.SemaphoreType.DMA
    vm = pltpu.VMEM
    hbm = pl.BlockSpec(memory_space=pltpu.HBM)
    zs, ys = PLANE - 1, COLS - 1
    pairs = [zs, ys, 3, 4, zs, zs, PLANE * ys, PLANE, PLANE, zs, PLANE * ys, zs, zs, ys, DP - 1]
    return pl.pallas_call(
        body,
        out_shape=(
            jax.ShapeDtypeStruct((128, 512), BF16),
            jax.ShapeDtypeStruct((128, 1024), BF16),
            jax.ShapeDtypeStruct((32, 512), F32),
        ),
        in_specs=[pl.BlockSpec(memory_space=pltpu.SMEM)] + [hbm] * 4,
        out_specs=tuple([pl.BlockSpec(memory_space=pltpu.VMEM)] * 3),
        scratch_shapes=[
            vm((128, 512), BF16), vm((128, 1024), BF16), vm((32, 512), BF16),
            vm((HEADS, 16, 128), BF16), vm((CTX, 16, 128), BF16),
            vm((PLANE, 128, 1024), BF16), vm((1024, 1024), BF16),
            vm((HEADS, BLK, 128), BF16), vm((PLANE, BLK, 128), BF16),
            vm((HEADS, 2, BLK, 128), BF16), vm((NQB, BLK, 128), BF16),
            vm((PLANE, BLK, 128), BF16), vm((PLANE, BLK, 128), BF16),
            vm((UNITS, BLK, KPQ * BLK), BF16),
            vm((PLANE, BLK, 128), BF16), vm((PLANE, BLK, 128), BF16),
            vm((PLANE, BLK, 128), BF16), vm((PLANE, BLK, 128), BF16),
            vm((ENTRIES, BLK, 128), F32), vm((ENTRIES + 1, BLK, 128), F32),
            vm((CTX, 2, BLK, 128), BF16), vm((COLS - 1, PLANE, 2, BLK, 128), BF16),
            vm((PLANE, 2, BLK, 128), BF16), vm((PLANE - 1, 2, BLK, 128), BF16),
            vm((HEADS, 2, BLK, 128), BF16),
            vm((COLS, PLANE, 16, 128), BF16), vm((COLS, PLANE, 16, 128), BF16),
            vm((PLANE, 16, 128), BF16), vm((PLANE, 16, 128), BF16),
            vm((16, 128), BF16), vm((DP, 16, 128), BF16),
            dma((4,)),
        ] + [dma((n,)) for n in pairs for _ in range(2)],
        compiler_params=pltpu.CompilerParams(
            collective_id=0, has_side_effects=True, vmem_limit_bytes=60 * 2**20
        ),
        name="attention_step",
    )(tab, queries, keyvals, out_weight, out_grad)


def solution(mesh):
    placed = (
        P(("dp", "ctx"), None),
        P(("dp", "ctx"), None),
        P("ctx", None),
        P(("dp", "ctx"), None),
        P("dp", None, None),
        P("dp", None),
        P("dp"),
    )
    return jax.shard_map(
        per_device,
        mesh=mesh,
        in_specs=placed,
        out_specs=(P(("dp", "ctx"), None), P(("dp", "ctx"), None), P("ctx", None)),
        check_vma=False,
    )
```

```python
import math

import jax
import jax.numpy as jnp
from jax import lax
from jax.experimental import pallas as pl
from jax.experimental.pallas import tpu as pltpu
from jax.sharding import PartitionSpec as P

HEADS = 8
HEAD_DIM = 64
BLK = 64
KPQ = 8
NQB = 64
CTX = 32
COLS = 4
LAG = 3
DP = 16
PLANE = 8
UNITS = 16
ENTRIES = UNITS * KPQ
FACTOR = 1.0 / math.sqrt(HEAD_DIM)
WG_SCALE = 1.0 / math.sqrt(128 * CTX * DP)
MESH = pl.DeviceIdType.MESH
BF16 = jnp.bfloat16
F32 = jnp.float32

T_LIST = 0
T_PERM = T_LIST + ENTRIES
T_SAME = T_PERM + ENTRIES
T_LAST = T_SAME + ENTRIES
T_COUNT = T_LAST + NQB
T_LENGTH = T_COUNT + UNITS


def low_half(shape):
    return lax.broadcasted_iota(jnp.int32, shape, 1) < HEAD_DIM


def pair_up(first, second, which):
    first, second = first.astype(F32), second.astype(F32)
    low = low_half(first.shape)
    if which == 0:
        return jnp.where(low, first, pltpu.roll(second, HEAD_DIM, 1))
    return jnp.where(low, pltpu.roll(first, HEAD_DIM, 1), second)


def dot(a, b, dims=((1,), (0,))):
    return lax.dot_general(a, b, (dims, ((), ())), preferred_element_type=F32)


def remote(src, dst, send, recv, **where):
    return pltpu.make_async_remote_copy(
        src_ref=src, dst_ref=dst, send_sem=send, recv_sem=recv,
        device_id=where, device_id_type=MESH,
    )


def body(tab, q_hbm, kv_hbm, w_hbm, og_hbm, dq_out, dkv_out, wg_out,
         q_ref, kv_ref, w_ref, w_tile, w_all, og_all, og_t, q_pack, q_all, kv_pack, kv_all,
         g_pack, g_all, p_all, o_pack, o_all, dq_pack, dq_all, entry_grads, sums,
         dkv_pack, dkv_y, dkv_mix, dkv_z, dkv_in, wg_pack, wg_in, wg_mid, wg_col, wg_last, wg_all,
         in_sem, w_s, w_r, wy_s, wy_r, og_s, og_r, oc_s, oc_r, q_s, q_r, kv_s, kv_r, kvy_s, kvy_r,
         g_s, g_r, o_s, o_r, dq_s, dq_r, dkvy_s, dkvy_r, dkv_s, dkv_r, b_s, b_r, by_s, by_r,
         c_s, c_r):
    dp = lax.axis_index("dp")
    me = lax.axis_index("ctx")
    col, z = me // PLANE, lax.rem(me, PLANE)
    part = lax.rem(dp, PLANE)
    base = dp - part
    x, core = part // 2, lax.rem(part, 2)
    partner = base + 2 * x + 1 - core
    col_peers = [lax.rem(col + i, COLS) for i in range(1, COLS)]
    dp_peers = [lax.rem(dp + i, DP) for i in range(1, DP)]
    z_peers = [lax.rem(z + i, PLANE) for i in range(1, PLANE)]
    x_peers = [lax.rem(x + i, 4) for i in range(1, 4)]
    here = part == z

    loads = [
        pltpu.make_async_copy(w_hbm, w_ref, in_sem.at[0]),
        pltpu.make_async_copy(og_hbm, og_all.at[part], in_sem.at[1]),
        pltpu.make_async_copy(q_hbm, q_ref, in_sem.at[2]),
        pltpu.make_async_copy(kv_hbm, kv_ref, in_sem.at[3]),
    ]
    for copy in loads:
        copy.start()

    barrier = pltpu.get_barrier_semaphore()

    def greet(**where):
        pl.semaphore_signal(barrier, inc=1, device_id=where, device_id_type=MESH)

    for peer in z_peers:
        greet(ctx=col * PLANE + peer)
    for peer in col_peers:
        greet(ctx=peer * PLANE + z)
    for peer in dp_peers:
        greet(dp=peer)
    for i in range(1, PLANE):
        other = lax.rem(part + i, PLANE)
        greet(dp=base + other, ctx=col * PLANE + part)
        greet(dp=base + other, ctx=col * PLANE + lax.rem(z + PLANE - other, PLANE))
    stays = part == 0

    @pl.when(jnp.logical_not(here))
    def _():
        greet(dp=dp, ctx=col * PLANE + part)

    @pl.when(jnp.logical_not(stays))
    def _():
        greet(dp=dp, ctx=col * PLANE + lax.rem(z + PLANE - part, PLANE))

    low16 = low_half((16, 128))
    low = low_half((BLK, 128))
    loads[0].wait()
    for head in range(HEADS):
        cols = slice(128 * (head // 2), 128 * (head // 2) + 128)
        w_tile[head] = pair_up(w_ref[:16, cols], w_ref[16:, cols], head % 2).astype(BF16)
    w_all[me] = w_tile[lax.rem(part + z, HEADS)]
    loads[2].wait()
    for head in range(HEADS):
        cols = slice(128 * (head // 2), 128 * (head // 2) + 128)
        q_pack[head] = pair_up(q_ref[:BLK, cols], q_ref[BLK:, cols], head % 2).astype(BF16)
    loads[3].wait()
    for head in range(HEADS):
        first = 128 * (head // 2)
        for half in range(2):
            rows = slice(BLK * half, BLK * half + BLK)
            kv_pack[head, half] = pair_up(
                kv_ref[rows, first:first + 128], kv_ref[rows, 512 + first:640 + first], head % 2
            ).astype(BF16)
    loads[1].wait()

    barrier_count = PLANE - 1 + COLS - 1 + DP - 1 + 2 * (PLANE - 1)
    barrier_count = barrier_count + jnp.where(here, 0, 1) + jnp.where(stays, 0, 1)
    pl.semaphore_wait(barrier, barrier_count)

    w_copies, wy_copies, og_copies, og_core, q_copies, kv_copies, kvy_copies = [], [], [], [], [], [], []

    def rank_rows(ref, rank):
        return ref.at[pl.ds(2 * rank, 2)]

    right, left = lax.rem(col + 1, COLS), lax.rem(col + COLS - 1, COLS)
    to_right, to_left = [], []

    def pass_on(rank, n, to, kept):
        rows = rank_rows(kv_all, rank)
        copy = remote(rows, rows, kvy_s.at[n], kvy_r.at[n], ctx=to * PLANE + z)
        copy.start()
        kept.append(copy)
        kvy_copies.append(copy)

    def down_column(i):
        rank = col * PLANE + lax.rem(z + PLANE - i, PLANE)
        pass_on(rank, 2 * i, right, to_right)
        pass_on(rank, 2 * i + 1, left, to_left)

    def across_column(i):
        at = lax.rem(z + PLANE - i, PLANE)
        if i % 2 == 0:
            to_right[i].wait_recv()
            pass_on(left * PLANE + at, 2 * PLANE + i, right, far)
        else:
            to_left[i].wait_recv()
            pass_on(right * PLANE + at, 2 * PLANE + i, left, far)

    far = []
    for i, peer in enumerate(z_peers):
        w_copies.append(
            remote(w_tile.at[lax.rem(part + peer, HEADS)], w_all.at[me], w_s.at[i], w_r.at[i],
                   ctx=col * PLANE + peer)
        )
        w_copies[i].start()
    mine = og_all.at[part]
    for i, peer in enumerate(x_peers):
        og_copies.append(remote(mine, mine, og_s.at[i], og_r.at[i], dp=base + 2 * peer + core))
        og_copies[i].start()
    for i, peer in enumerate(z_peers):
        copy = remote(kv_pack.at[peer], rank_rows(kv_all, me), kv_s.at[i], kv_r.at[i],
                      ctx=col * PLANE + peer)
        copy.start()
        kv_copies.append(copy)
    kv_all[pl.ds(2 * me, 2)] = kv_pack[z]
    down_column(0)
    og_core.append(remote(mine, mine, oc_s.at[3], oc_r.at[3], dp=partner))
    og_core[0].start()
    for copy in w_copies:
        copy.wait()
    for j, peer in enumerate(col_peers):
        rows = w_all.at[pl.ds(col * PLANE, PLANE)]
        copy = remote(rows, rows, wy_s.at[j], wy_r.at[j], ctx=peer * PLANE + z)
        copy.start()
        wy_copies.append(copy)
    for i, peer in enumerate(z_peers):
        q_copies.append(
            remote(q_pack.at[peer], q_all.at[z], q_s.at[i], q_r.at[i], ctx=col * PLANE + peer)
        )
        q_copies[i].start()
    q_all[z] = q_pack[z]

    for i in range(1, PLANE):
        kv_copies[i - 1].wait_recv()
        down_column(i)
        if i > LAG:
            across_column(i - LAG - 1)

    for i in range(3):
        og_copies[i].wait_recv()
        slot = 2 * lax.rem(x + 3 - i, 4) + core
        copy = remote(og_all.at[slot], og_all.at[slot], oc_s.at[i], oc_r.at[i], dp=partner)
        copy.start()
        og_core.append(copy)
    for copy in wy_copies:
        copy.wait()
    for copy in og_core:
        copy.wait_recv()

    weight = w_all[...].reshape(CTX, 1, 16, 128)
    none = jnp.zeros_like(weight)
    low4 = lax.broadcasted_iota(jnp.int32, weight.shape, 3) < HEAD_DIM
    weight = jnp.concatenate(
        [jnp.where(low4, weight, none), jnp.where(low4, none, weight)], axis=1
    ).reshape(CTX * 32, 128)
    for s in range(PLANE):
        grad = dot(og_all[s], weight)
        grad = grad + pltpu.roll(grad, HEAD_DIM, 1)
        g_pack[s] = jnp.where(low, grad[:BLK], grad[BLK:]).astype(BF16)
    g_copies = []
    head = lax.rem(part + z, HEADS)
    for i in range(PLANE):
        peer = lax.rem(part + i, PLANE)
        copy = remote(g_pack.at[peer], g_all.at[z], g_s.at[i], g_r.at[z],
                      dp=base + peer, ctx=col * PLANE + head)
        g_copies.append(copy)
        if i:
            copy.start()
        else:
            pl.when(jnp.logical_not(stays))(copy.start)

            @pl.when(stays)
            def _():
                g_all[z] = g_pack[part]

    for i in range(PLANE - LAG - 1, PLANE):
        across_column(i)
    for s in range(PLANE):
        og_t[:, 128 * s:128 * s + 128] = og_all[s].T
    for i in range(PLANE):
        (to_left if i % 2 == 0 else to_right)[i].wait_recv()
    for copy in q_copies + far:
        copy.wait_recv()

    length = tab[T_LENGTH]
    lane = lax.broadcasted_iota(jnp.int32, (1, 128), 1)
    row = lax.broadcasted_iota(jnp.int32, (BLK, 1), 0)
    entry = lax.broadcasted_iota(jnp.int32, (1, KPQ * BLK), 1) // BLK

    def listed(u):
        blocks = [tab[T_LIST + u * KPQ + j] for j in range(KPQ)]
        return blocks, jnp.concatenate([kv_all[b] for b in blocks], axis=0)

    def forward(zp, carry):
        query = q_all[zp].astype(F32) * FACTOR
        outs = []
        for p in range(2):
            u = 2 * zp + p
            blocks, keyval = listed(u)
            left = query if p == 0 else pltpu.roll(query, HEAD_DIM, 1)
            scores = dot(jnp.where(low, left, 0.0).astype(BF16), keyval, ((1,), (1,)))
            place = jnp.concatenate(
                [
                    jnp.where(lane < BLK, blocks[j] * BLK + lane, blocks[j + 1] * BLK + lane - BLK)
                    for j in range(0, KPQ, 2)
                ],
                axis=1,
            )
            own = (col * UNITS + u) * BLK + row
            allowed = (entry < tab[T_COUNT + u]) & ((place < length) | (place == own))
            scores = jnp.where(allowed, scores, -jnp.inf)
            exponent = jnp.exp(scores - jnp.max(scores, axis=1, keepdims=True))
            probs = exponent * (1.0 / jnp.sum(exponent, axis=1, keepdims=True))
            probs = probs.astype(BF16)
            p_all[u] = probs
            outs.append(dot(probs, keyval) * (own < length).astype(F32))
        o_pack[zp] = pair_up(outs[0], outs[1], 1).astype(BF16)
        return carry

    lax.fori_loop(0, PLANE, forward, 0, unroll=2)

    o_copies = []
    for i in range(PLANE):
        peer = lax.rem(z + i, PLANE)
        copy = remote(o_pack.at[peer], o_all.at[part], o_s.at[i], o_r.at[part],
                      dp=base + z, ctx=col * PLANE + peer)
        o_copies.append(copy)
        if i:
            copy.start()
        else:
            pl.when(jnp.logical_not(here))(copy.start)

            @pl.when(here)
            def _():
                o_all[part] = o_pack[z]

    def arrived(dst, sem):
        remote(dst, dst, sem, sem, dp=dp, ctx=me).wait_recv()

    for i in range(1, PLANE):
        slot = lax.rem(z + i, PLANE)
        arrived(g_all.at[slot], g_r.at[slot])

    @pl.when(jnp.logical_not(stays))
    def _():
        arrived(g_all.at[z], g_r.at[z])

    def backward(zp, carry):
        query = q_all[zp].astype(F32) * FACTOR
        grads = g_all[zp].astype(F32)
        outs = []
        for p in range(2):
            u = 2 * zp + p
            _, keyval = listed(u)
            valid = ((col * UNITS + u) * BLK + row < length).astype(F32)
            if p == 0:
                top, bottom = query, pltpu.roll(grads, HEAD_DIM, 1)
            else:
                top, bottom = pltpu.roll(query, HEAD_DIM, 1), grads
            top = jnp.where(low, top, 0.0).astype(BF16)
            bottom = jnp.where(low, 0.0, bottom * valid).astype(BF16)
            prob_grad = dot(bottom, keyval, ((1,), (1,)))
            probs16 = p_all[u]
            probs = probs16.astype(F32)
            delta = jnp.sum(probs * prob_grad, axis=1, keepdims=True)
            score_grad = (probs * (prob_grad - delta)).astype(BF16)
            outs.append(dot(score_grad, keyval) * FACTOR)
            stacked = jnp.concatenate([score_grad, probs16], axis=0)
            grad = dot(stacked, jnp.concatenate([top, bottom], axis=0), ((0,), (0,)))
            for j in range(KPQ):
                entry_grads[u * KPQ + j] = grad[j * BLK:(j + 1) * BLK]
        dq_pack[zp] = pair_up(outs[0], outs[1], 0).astype(BF16)
        return carry

    lax.fori_loop(0, PLANE, backward, 0, unroll=2)

    dq_copies = []
    for i, peer in enumerate(z_peers):
        copy = remote(dq_pack.at[peer], dq_all.at[z], dq_s.at[i], dq_r.at[i], ctx=col * PLANE + peer)
        copy.start()
        dq_copies.append(copy)
    dq_all[z] = dq_pack[z]

    sums[ENTRIES] = jnp.zeros((BLK, 128), F32)

    def accumulate(t, total):
        total = entry_grads[tab[T_PERM + t]] + total * tab[T_SAME + t].astype(F32)
        sums[t] = total
        return total

    lax.fori_loop(0, ENTRIES, accumulate, jnp.zeros((BLK, 128), F32), unroll=16)

    def pack(c):
        for half in range(2):
            dkv_pack[c, half] = sums[tab[T_LAST + 2 * c + half]].astype(BF16)

    dkvy_copies, dkv_copies = [], []

    opposite = lax.rem(col + 2, COLS)
    far_copies, mixed_copies = [], []

    def step_dkv(i, n, src, slot, to):
        zc = lax.rem(z + 1 + i, PLANE)
        copy = remote(src, dkv_y.at[slot, zc], dkvy_s.at[3 * i + n], dkvy_r.at[3 * i + n],
                      ctx=to * PLANE + z)
        copy.start()
        return copy

    def send_dkv(i):
        zc = lax.rem(z + 1 + i, PLANE)
        ahead, behind = (right, left) if i % 2 == 0 else (left, right)
        for y in (opposite, behind, ahead):
            pack(y * PLANE + zc)
        far_copies.append(step_dkv(i, 0, dkv_pack.at[opposite * PLANE + zc], 2, ahead))
        dkvy_copies.append(step_dkv(i, 1, dkv_pack.at[behind * PLANE + zc], 0, behind))

    def mix_dkv(i):
        zc = lax.rem(z + 1 + i, PLANE)
        ahead = right if i % 2 == 0 else left
        far_copies[i].wait_recv()
        total = dkv_pack[ahead * PLANE + zc].astype(F32) + dkv_y[2, zc].astype(F32)
        dkv_mix[i] = total.astype(BF16)
        mixed_copies.append(step_dkv(i, 2, dkv_mix.at[i], 1, ahead))

    for i in range(2):
        send_dkv(i)

    for i in range(1, PLANE):
        slot = lax.rem(part + i, PLANE)
        arrived(o_all.at[slot], o_r.at[slot])

    @pl.when(jnp.logical_not(here))
    def _():
        arrived(o_all.at[part], o_r.at[part])

    attention = o_all[...].reshape(PLANE, 1, BLK, 128)
    none = jnp.zeros_like(attention)
    low4 = lax.broadcasted_iota(jnp.int32, attention.shape, 3) < HEAD_DIM
    attention = jnp.concatenate(
        [jnp.where(low4, attention, none), jnp.where(low4, none, attention)], axis=1
    ).reshape(PLANE * 128, 128)
    for c in range(0, CTX, 8):
        grad = dot(og_t[32 * c:32 * c + 256], attention)
        grad = ((grad + pltpu.roll(grad, HEAD_DIM, 1)) * WG_SCALE).reshape(8, 2, 16, 128)
        for k in range(8):
            wg_pack[c // PLANE, k] = jnp.where(low16, grad[k, 0], grad[k, 1]).astype(BF16)
    by_copies, b_copies, c_copies = [], [], []
    for j, peer in enumerate(col_peers):
        copy = remote(wg_pack.at[peer], wg_in.at[col], by_s.at[j], by_r.at[j], ctx=peer * PLANE + z)
        copy.start()
        by_copies.append(copy)
    wg_in[col] = wg_pack[col]

    for i in range(2, PLANE):
        send_dkv(i)
        mix_dkv(i - 2)

    for copy in by_copies:
        copy.wait()
    wg_mid[...] = sum(wg_in[i].astype(F32) for i in range(COLS)).astype(BF16)
    for i, peer in enumerate(z_peers):
        copy = remote(wg_mid.at[peer], wg_col.at[z], b_s.at[i], b_r.at[i], ctx=col * PLANE + peer)
        copy.start()
        b_copies.append(copy)
    wg_col[z] = wg_mid[z]

    for i in range(PLANE):
        zc = lax.rem(z + 1 + i, PLANE)
        pack(col * PLANE + zc)
        if i < 2:
            mix_dkv(PLANE - 2 + i)
        dkvy_copies[i].wait_recv()
        mixed_copies[i].wait_recv()
        total = dkv_pack[col * PLANE + zc].astype(F32)
        for j in range(2):
            total = total + dkv_y[j, zc].astype(F32)
        if i == PLANE - 1:
            dkv_in[z] = total.astype(BF16)
        else:
            dkv_z[i] = total.astype(BF16)
            copy = remote(dkv_z.at[i], dkv_in.at[z], dkv_s.at[i], dkv_r.at[i], ctx=col * PLANE + zc)
            copy.start()
            dkv_copies.append(copy)
        if i == 1:
            for copy in b_copies:
                copy.wait()
            wg_last[...] = sum(wg_col[k].astype(F32) for k in range(PLANE)).astype(BF16)
            for k, peer in enumerate(dp_peers):
                copy = remote(wg_last, wg_all.at[dp], c_s.at[k], c_r.at[k], dp=peer)
                copy.start()
                c_copies.append(copy)
            wg_all[dp] = wg_last[...]

    for copy in dq_copies:
        copy.wait()
    for c in range(4):
        for half in range(2):
            dq_out[BLK * half:BLK * half + BLK, 128 * c:128 * c + 128] = pair_up(
                dq_all[2 * c], dq_all[2 * c + 1], half
            ).astype(BF16)

    for copy in c_copies:
        copy.wait()
    for c in range(4):
        even = wg_all[2 * c].astype(F32) + wg_all[PLANE + 2 * c].astype(F32)
        odd_ = wg_all[2 * c + 1].astype(F32) + wg_all[PLANE + 2 * c + 1].astype(F32)
        for half in range(2):
            wg_out[16 * half:16 * half + 16, 128 * c:128 * c + 128] = pair_up(even, odd_, half)

    for copy in dkv_copies:
        copy.wait()
    for c in range(4):
        for half in range(2):
            rows = slice(BLK * half, BLK * half + BLK)
            even, odd_ = dkv_in[2 * c, half], dkv_in[2 * c + 1, half]
            dkv_out[rows, 128 * c:128 * c + 128] = pair_up(even, odd_, 0).astype(BF16)
            dkv_out[rows, 512 + 128 * c:640 + 128 * c] = pair_up(even, odd_, 1).astype(BF16)

    for copy in (og_copies + og_core + q_copies + kv_copies + kvy_copies + dkvy_copies + far_copies
                 + mixed_copies + g_copies[1:] + o_copies[1:]):
        copy.wait_send()

    @pl.when(jnp.logical_not(here))
    def _():
        o_copies[0].wait_send()

    @pl.when(jnp.logical_not(stays))
    def _():
        g_copies[0].wait_send()


def table(block_list, counts, length, first):
    mine = lax.dynamic_slice_in_dim(block_list, first, UNITS, 0).reshape(ENTRIES)
    ids = jnp.arange(ENTRIES, dtype=jnp.int32)
    key = mine * ENTRIES + ids
    place = jnp.sum((key[None, :] < key[:, None]).astype(jnp.int32), axis=1)
    at = place[None, :] == ids[:, None]
    perm = jnp.sum(jnp.where(at, ids[None, :], 0), axis=1)
    same = (mine[None, :] == mine[:, None]) & (ids[None, :] < ids[:, None])
    later = jnp.max(same.astype(jnp.int32), axis=1)
    go_on = jnp.sum(jnp.where(at, later[None, :], 0), axis=1)
    blocks = jnp.arange(NQB, dtype=jnp.int32)
    upto = jnp.sum((mine[None, :] <= blocks[:, None]).astype(jnp.int32), axis=1)
    named = jnp.max((mine[None, :] == blocks[:, None]).astype(jnp.int32), axis=1)
    last = jnp.where(named > 0, upto - 1, ENTRIES)
    mine_counts = lax.dynamic_slice_in_dim(counts, first, UNITS, 0)
    return jnp.concatenate([mine, perm, go_on, last, mine_counts, length])


def per_device(queries, keyvals, out_weight, out_grad, block_lists, block_counts, seq_lengths):
    first = (lax.axis_index("ctx") // PLANE) * UNITS
    tab = table(block_lists[0], block_counts[0], seq_lengths, first)
    dma = pltpu.SemaphoreType.DMA
    vm = pltpu.VMEM
    hbm = pl.BlockSpec(memory_space=pltpu.HBM)
    zs, ys = PLANE - 1, COLS - 1
    pairs = [zs, ys, 3, 4, zs, zs, PLANE * ys, PLANE, PLANE, zs, PLANE * ys, zs, zs, ys, DP - 1]
    return pl.pallas_call(
        body,
        out_shape=(
            jax.ShapeDtypeStruct((128, 512), BF16),
            jax.ShapeDtypeStruct((128, 1024), BF16),
            jax.ShapeDtypeStruct((32, 512), F32),
        ),
        in_specs=[pl.BlockSpec(memory_space=pltpu.SMEM)] + [hbm] * 4,
        out_specs=tuple([pl.BlockSpec(memory_space=pltpu.VMEM)] * 3),
        scratch_shapes=[
            vm((128, 512), BF16), vm((128, 1024), BF16), vm((32, 512), BF16),
            vm((HEADS, 16, 128), BF16), vm((CTX, 16, 128), BF16),
            vm((PLANE, 128, 1024), BF16), vm((1024, 1024), BF16),
            vm((HEADS, BLK, 128), BF16), vm((PLANE, BLK, 128), BF16),
            vm((HEADS, 2, BLK, 128), BF16), vm((NQB, BLK, 128), BF16),
            vm((PLANE, BLK, 128), BF16), vm((PLANE, BLK, 128), BF16),
            vm((UNITS, BLK, KPQ * BLK), BF16),
            vm((PLANE, BLK, 128), BF16), vm((PLANE, BLK, 128), BF16),
            vm((PLANE, BLK, 128), BF16), vm((PLANE, BLK, 128), BF16),
            vm((ENTRIES, BLK, 128), F32), vm((ENTRIES + 1, BLK, 128), F32),
            vm((CTX, 2, BLK, 128), BF16), vm((COLS - 1, PLANE, 2, BLK, 128), BF16),
            vm((PLANE, 2, BLK, 128), BF16), vm((PLANE - 1, 2, BLK, 128), BF16),
            vm((HEADS, 2, BLK, 128), BF16),
            vm((COLS, PLANE, 16, 128), BF16), vm((COLS, PLANE, 16, 128), BF16),
            vm((PLANE, 16, 128), BF16), vm((PLANE, 16, 128), BF16),
            vm((16, 128), BF16), vm((DP, 16, 128), BF16),
            dma((4,)),
        ] + [dma((n,)) for n in pairs for _ in range(2)],
        compiler_params=pltpu.CompilerParams(
            collective_id=0, has_side_effects=True, vmem_limit_bytes=60 * 2**20
        ),
        name="attention_step",
    )(tab, queries, keyvals, out_weight, out_grad)


def solution(mesh):
    placed = (
        P(("dp", "ctx"), None),
        P(("dp", "ctx"), None),
        P("ctx", None),
        P(("dp", "ctx"), None),
        P("dp", None, None),
        P("dp", None),
        P("dp"),
    )
    return jax.shard_map(
        per_device,
        mesh=mesh,
        in_specs=placed,
        out_specs=(P(("dp", "ctx"), None), P(("dp", "ctx"), None), P("ctx", None)),
        check_vma=False,
    )
```

```python
import math

import jax
import jax.numpy as jnp
from jax import lax
from jax.experimental import pallas as pl
from jax.experimental.pallas import tpu as pltpu
from jax.sharding import PartitionSpec as P

HEADS = 8
HEAD_DIM = 64
BLK = 64
KPQ = 8
NQB = 64
CTX = 32
COLS = 4
LAG = 3
DP = 16
PLANE = 8
UNITS = 16
ENTRIES = UNITS * KPQ
FACTOR = 1.0 / math.sqrt(HEAD_DIM)
WG_SCALE = 1.0 / math.sqrt(128 * CTX * DP)
MESH = pl.DeviceIdType.MESH
BF16 = jnp.bfloat16
F32 = jnp.float32

T_LIST = 0
T_PERM = T_LIST + ENTRIES
T_SAME = T_PERM + ENTRIES
T_LAST = T_SAME + ENTRIES
T_COUNT = T_LAST + NQB
T_LENGTH = T_COUNT + UNITS


def low_half(shape):
    return lax.broadcasted_iota(jnp.int32, shape, 1) < HEAD_DIM


def pair_up(first, second, which):
    first, second = first.astype(F32), second.astype(F32)
    low = low_half(first.shape)
    if which == 0:
        return jnp.where(low, first, pltpu.roll(second, HEAD_DIM, 1))
    return jnp.where(low, pltpu.roll(first, HEAD_DIM, 1), second)


def dot(a, b, dims=((1,), (0,))):
    return lax.dot_general(a, b, (dims, ((), ())), preferred_element_type=F32)


def remote(src, dst, send, recv, **where):
    return pltpu.make_async_remote_copy(
        src_ref=src, dst_ref=dst, send_sem=send, recv_sem=recv,
        device_id=where, device_id_type=MESH,
    )


def body(tab, q_hbm, kv_hbm, w_hbm, og_hbm, dq_out, dkv_out, wg_out,
         q_ref, kv_ref, w_ref, w_tile, w_all, og_all, og_t, q_pack, q_all, kv_pack, kv_all,
         g_pack, g_all, p_all, o_pack, o_all, dq_pack, dq_all, entry_grads, sums,
         dkv_pack, dkv_y, dkv_mix, dkv_z, dkv_in, wg_pack, wg_in, wg_mid, wg_col, wg_last, wg_all,
         in_sem, w_s, w_r, wy_s, wy_r, og_s, og_r, oc_s, oc_r, q_s, q_r, kv_s, kv_r, kvy_s, kvy_r,
         g_s, g_r, o_s, o_r, dq_s, dq_r, dkvy_s, dkvy_r, dkv_s, dkv_r, b_s, b_r, by_s, by_r,
         c_s, c_r):
    dp = lax.axis_index("dp")
    me = lax.axis_index("ctx")
    col, z = me // PLANE, lax.rem(me, PLANE)
    part = lax.rem(dp, PLANE)
    base = dp - part
    x, core = part // 2, lax.rem(part, 2)
    partner = base + 2 * x + 1 - core
    col_peers = [lax.rem(col + i, COLS) for i in range(1, COLS)]
    dp_peers = [lax.rem(dp + i, DP) for i in range(1, DP)]
    z_peers = [lax.rem(z + i, PLANE) for i in range(1, PLANE)]
    x_peers = [lax.rem(x + i, 4) for i in range(1, 4)]
    here = part == z

    loads = [
        pltpu.make_async_copy(w_hbm, w_ref, in_sem.at[0]),
        pltpu.make_async_copy(og_hbm, og_all.at[part], in_sem.at[1]),
        pltpu.make_async_copy(q_hbm, q_ref, in_sem.at[2]),
        pltpu.make_async_copy(kv_hbm, kv_ref, in_sem.at[3]),
    ]
    for copy in loads:
        copy.start()

    barrier = pltpu.get_barrier_semaphore()

    def greet(**where):
        pl.semaphore_signal(barrier, inc=1, device_id=where, device_id_type=MESH)

    for peer in z_peers:
        greet(ctx=col * PLANE + peer)
    for peer in col_peers:
        greet(ctx=peer * PLANE + z)
    for peer in dp_peers:
        greet(dp=peer)
    for i in range(1, PLANE):
        other = lax.rem(part + i, PLANE)
        greet(dp=base + other, ctx=col * PLANE + part)
        greet(dp=base + other, ctx=col * PLANE + lax.rem(z + PLANE - other, PLANE))
    stays = part == 0

    @pl.when(jnp.logical_not(here))
    def _():
        greet(dp=dp, ctx=col * PLANE + part)

    @pl.when(jnp.logical_not(stays))
    def _():
        greet(dp=dp, ctx=col * PLANE + lax.rem(z + PLANE - part, PLANE))

    low16 = low_half((16, 128))
    low = low_half((BLK, 128))
    loads[0].wait()
    for head in range(HEADS):
        cols = slice(128 * (head // 2), 128 * (head // 2) + 128)
        w_tile[head] = pair_up(w_ref[:16, cols], w_ref[16:, cols], head % 2).astype(BF16)
    w_all[me] = w_tile[lax.rem(part + z, HEADS)]
    loads[2].wait()
    for head in range(HEADS):
        cols = slice(128 * (head // 2), 128 * (head // 2) + 128)
        q_pack[head] = pair_up(q_ref[:BLK, cols], q_ref[BLK:, cols], head % 2).astype(BF16)
    loads[3].wait()
    for head in range(HEADS):
        first = 128 * (head // 2)
        for half in range(2):
            rows = slice(BLK * half, BLK * half + BLK)
            kv_pack[head, half] = pair_up(
                kv_ref[rows, first:first + 128], kv_ref[rows, 512 + first:640 + first], head % 2
            ).astype(BF16)
    loads[1].wait()

    barrier_count = PLANE - 1 + COLS - 1 + DP - 1 + 2 * (PLANE - 1)
    barrier_count = barrier_count + jnp.where(here, 0, 1) + jnp.where(stays, 0, 1)
    pl.semaphore_wait(barrier, barrier_count)

    w_copies, wy_copies, og_copies, og_core, q_copies, kv_copies, kvy_copies = [], [], [], [], [], [], []

    def rank_rows(ref, rank):
        return ref.at[pl.ds(2 * rank, 2)]

    right, left = lax.rem(col + 1, COLS), lax.rem(col + COLS - 1, COLS)
    to_right, to_left = [], []

    def pass_on(rank, n, to, kept):
        rows = rank_rows(kv_all, rank)
        copy = remote(rows, rows, kvy_s.at[n], kvy_r.at[n], ctx=to * PLANE + z)
        copy.start()
        kept.append(copy)
        kvy_copies.append(copy)

    def down_column(i):
        rank = col * PLANE + lax.rem(z + PLANE - i, PLANE)
        pass_on(rank, 2 * i, right, to_right)
        pass_on(rank, 2 * i + 1, left, to_left)

    def across_column(i):
        at = lax.rem(z + PLANE - i, PLANE)
        if i % 2 == 0:
            to_right[i].wait_recv()
            pass_on(left * PLANE + at, 2 * PLANE + i, right, far)
        else:
            to_left[i].wait_recv()
            pass_on(right * PLANE + at, 2 * PLANE + i, left, far)

    far = []
    for i, peer in enumerate(z_peers):
        w_copies.append(
            remote(w_tile.at[lax.rem(part + peer, HEADS)], w_all.at[me], w_s.at[i], w_r.at[i],
                   ctx=col * PLANE + peer)
        )
        w_copies[i].start()
    mine = og_all.at[part]
    for i, peer in enumerate(x_peers):
        og_copies.append(remote(mine, mine, og_s.at[i], og_r.at[i], dp=base + 2 * peer + core))
        og_copies[i].start()
    for i, peer in enumerate(z_peers):
        copy = remote(kv_pack.at[peer], rank_rows(kv_all, me), kv_s.at[i], kv_r.at[i],
                      ctx=col * PLANE + peer)
        copy.start()
        kv_copies.append(copy)
    kv_all[pl.ds(2 * me, 2)] = kv_pack[z]
    down_column(0)
    og_core.append(remote(mine, mine, oc_s.at[3], oc_r.at[3], dp=partner))
    og_core[0].start()
    for copy in w_copies:
        copy.wait()
    for j, peer in enumerate(col_peers):
        rows = w_all.at[pl.ds(col * PLANE, PLANE)]
        copy = remote(rows, rows, wy_s.at[j], wy_r.at[j], ctx=peer * PLANE + z)
        copy.start()
        wy_copies.append(copy)
    for i, peer in enumerate(z_peers):
        q_copies.append(
            remote(q_pack.at[peer], q_all.at[z], q_s.at[i], q_r.at[i], ctx=col * PLANE + peer)
        )
        q_copies[i].start()
    q_all[z] = q_pack[z]

    for i in range(1, PLANE):
        kv_copies[i - 1].wait_recv()
        down_column(i)
        if i > LAG:
            across_column(i - LAG - 1)

    for i in range(3):
        og_copies[i].wait_recv()
        slot = 2 * lax.rem(x + 3 - i, 4) + core
        copy = remote(og_all.at[slot], og_all.at[slot], oc_s.at[i], oc_r.at[i], dp=partner)
        copy.start()
        og_core.append(copy)
    for copy in wy_copies:
        copy.wait()
    for copy in og_core:
        copy.wait_recv()

    weight = w_all[...].reshape(CTX, 1, 16, 128)
    none = jnp.zeros_like(weight)
    low4 = lax.broadcasted_iota(jnp.int32, weight.shape, 3) < HEAD_DIM
    weight = jnp.concatenate(
        [jnp.where(low4, weight, none), jnp.where(low4, none, weight)], axis=1
    ).reshape(CTX * 32, 128)
    for s in range(PLANE):
        grad = dot(og_all[s], weight)
        grad = grad + pltpu.roll(grad, HEAD_DIM, 1)
        g_pack[s] = jnp.where(low, grad[:BLK], grad[BLK:]).astype(BF16)
    g_copies = []
    head = lax.rem(part + z, HEADS)
    for i in range(PLANE):
        peer = lax.rem(part + i, PLANE)
        copy = remote(g_pack.at[peer], g_all.at[z], g_s.at[i], g_r.at[z],
                      dp=base + peer, ctx=col * PLANE + head)
        g_copies.append(copy)
        if i:
            copy.start()
        else:
            pl.when(jnp.logical_not(stays))(copy.start)

            @pl.when(stays)
            def _():
                g_all[z] = g_pack[part]

    for i in range(PLANE - LAG - 1, PLANE):
        across_column(i)
    for s in range(PLANE):
        og_t[:, 128 * s:128 * s + 128] = og_all[s].T
    for i in range(PLANE):
        (to_left if i % 2 == 0 else to_right)[i].wait_recv()
    for copy in q_copies + far:
        copy.wait_recv()

    length = tab[T_LENGTH]
    lane = lax.broadcasted_iota(jnp.int32, (1, 128), 1)
    row = lax.broadcasted_iota(jnp.int32, (BLK, 1), 0)
    entry = lax.broadcasted_iota(jnp.int32, (1, KPQ * BLK), 1) // BLK

    def listed(u):
        blocks = [tab[T_LIST + u * KPQ + j] for j in range(KPQ)]
        return blocks, jnp.concatenate([kv_all[b] for b in blocks], axis=0)

    def forward(zp, carry):
        query = q_all[zp].astype(F32) * FACTOR
        outs = []
        for p in range(2):
            u = 2 * zp + p
            blocks, keyval = listed(u)
            left = query if p == 0 else pltpu.roll(query, HEAD_DIM, 1)
            scores = dot(jnp.where(low, left, 0.0).astype(BF16), keyval, ((1,), (1,)))
            place = jnp.concatenate(
                [
                    jnp.where(lane < BLK, blocks[j] * BLK + lane, blocks[j + 1] * BLK + lane - BLK)
                    for j in range(0, KPQ, 2)
                ],
                axis=1,
            )
            own = (col * UNITS + u) * BLK + row
            allowed = (entry < tab[T_COUNT + u]) & ((place < length) | (place == own))
            scores = jnp.where(allowed, scores, -jnp.inf)
            exponent = jnp.exp(scores - jnp.max(scores, axis=1, keepdims=True))
            probs = exponent * (1.0 / jnp.sum(exponent, axis=1, keepdims=True))
            probs = probs.astype(BF16)
            p_all[u] = probs
            outs.append(dot(probs, keyval) * (own < length).astype(F32))
        o_pack[zp] = pair_up(outs[0], outs[1], 1).astype(BF16)
        return carry

    lax.fori_loop(0, PLANE, forward, 0, unroll=4)

    o_copies = []
    for i in range(PLANE):
        peer = lax.rem(z + i, PLANE)
        copy = remote(o_pack.at[peer], o_all.at[part], o_s.at[i], o_r.at[part],
                      dp=base + z, ctx=col * PLANE + peer)
        o_copies.append(copy)
        if i:
            copy.start()
        else:
            pl.when(jnp.logical_not(here))(copy.start)

            @pl.when(here)
            def _():
                o_all[part] = o_pack[z]

    def arrived(dst, sem):
        remote(dst, dst, sem, sem, dp=dp, ctx=me).wait_recv()

    for i in range(1, PLANE):
        slot = lax.rem(z + i, PLANE)
        arrived(g_all.at[slot], g_r.at[slot])

    @pl.when(jnp.logical_not(stays))
    def _():
        arrived(g_all.at[z], g_r.at[z])

    def backward(zp, carry):
        query = q_all[zp].astype(F32) * FACTOR
        grads = g_all[zp].astype(F32)
        outs = []
        for p in range(2):
            u = 2 * zp + p
            _, keyval = listed(u)
            valid = ((col * UNITS + u) * BLK + row < length).astype(F32)
            if p == 0:
                top, bottom = query, pltpu.roll(grads, HEAD_DIM, 1)
            else:
                top, bottom = pltpu.roll(query, HEAD_DIM, 1), grads
            top = jnp.where(low, top, 0.0).astype(BF16)
            bottom = jnp.where(low, 0.0, bottom * valid).astype(BF16)
            prob_grad = dot(bottom, keyval, ((1,), (1,)))
            probs16 = p_all[u]
            probs = probs16.astype(F32)
            delta = jnp.sum(probs * prob_grad, axis=1, keepdims=True)
            score_grad = (probs * (prob_grad - delta)).astype(BF16)
            outs.append(dot(score_grad, keyval) * FACTOR)
            stacked = jnp.concatenate([score_grad, probs16], axis=0)
            grad = dot(stacked, jnp.concatenate([top, bottom], axis=0), ((0,), (0,)))
            for j in range(KPQ):
                entry_grads[u * KPQ + j] = grad[j * BLK:(j + 1) * BLK]
        dq_pack[zp] = pair_up(outs[0], outs[1], 0).astype(BF16)
        return carry

    lax.fori_loop(0, PLANE, backward, 0, unroll=4)

    dq_copies = []
    for i, peer in enumerate(z_peers):
        copy = remote(dq_pack.at[peer], dq_all.at[z], dq_s.at[i], dq_r.at[i], ctx=col * PLANE + peer)
        copy.start()
        dq_copies.append(copy)
    dq_all[z] = dq_pack[z]

    sums[ENTRIES] = jnp.zeros((BLK, 128), F32)

    def accumulate(t, total):
        total = entry_grads[tab[T_PERM + t]] + total * tab[T_SAME + t].astype(F32)
        sums[t] = total
        return total

    lax.fori_loop(0, ENTRIES, accumulate, jnp.zeros((BLK, 128), F32), unroll=16)

    def pack(c):
        for half in range(2):
            dkv_pack[c, half] = sums[tab[T_LAST + 2 * c + half]].astype(BF16)

    dkvy_copies, dkv_copies = [], []

    opposite = lax.rem(col + 2, COLS)
    far_copies, mixed_copies = [], []

    def step_dkv(i, n, src, slot, to):
        zc = lax.rem(z + 1 + i, PLANE)
        copy = remote(src, dkv_y.at[slot, zc], dkvy_s.at[3 * i + n], dkvy_r.at[3 * i + n],
                      ctx=to * PLANE + z)
        copy.start()
        return copy

    def send_dkv(i):
        zc = lax.rem(z + 1 + i, PLANE)
        ahead, behind = (right, left) if i % 2 == 0 else (left, right)
        for y in (opposite, behind, ahead):
            pack(y * PLANE + zc)
        far_copies.append(step_dkv(i, 0, dkv_pack.at[opposite * PLANE + zc], 2, ahead))
        dkvy_copies.append(step_dkv(i, 1, dkv_pack.at[behind * PLANE + zc], 0, behind))

    def mix_dkv(i):
        zc = lax.rem(z + 1 + i, PLANE)
        ahead = right if i % 2 == 0 else left
        far_copies[i].wait_recv()
        total = dkv_pack[ahead * PLANE + zc].astype(F32) + dkv_y[2, zc].astype(F32)
        dkv_mix[i] = total.astype(BF16)
        mixed_copies.append(step_dkv(i, 2, dkv_mix.at[i], 1, ahead))

    for i in range(2):
        send_dkv(i)

    for i in range(1, PLANE):
        slot = lax.rem(part + i, PLANE)
        arrived(o_all.at[slot], o_r.at[slot])

    @pl.when(jnp.logical_not(here))
    def _():
        arrived(o_all.at[part], o_r.at[part])

    attention = o_all[...].reshape(PLANE, 1, BLK, 128)
    none = jnp.zeros_like(attention)
    low4 = lax.broadcasted_iota(jnp.int32, attention.shape, 3) < HEAD_DIM
    attention = jnp.concatenate(
        [jnp.where(low4, attention, none), jnp.where(low4, none, attention)], axis=1
    ).reshape(PLANE * 128, 128)
    for c in range(0, CTX, 8):
        grad = dot(og_t[32 * c:32 * c + 256], attention)
        grad = ((grad + pltpu.roll(grad, HEAD_DIM, 1)) * WG_SCALE).reshape(8, 2, 16, 128)
        for k in range(8):
            wg_pack[c // PLANE, k] = jnp.where(low16, grad[k, 0], grad[k, 1]).astype(BF16)
    by_copies, b_copies, c_copies = [], [], []
    for j, peer in enumerate(col_peers):
        copy = remote(wg_pack.at[peer], wg_in.at[col], by_s.at[j], by_r.at[j], ctx=peer * PLANE + z)
        copy.start()
        by_copies.append(copy)
    wg_in[col] = wg_pack[col]

    for i in range(2, PLANE):
        send_dkv(i)
        mix_dkv(i - 2)

    for copy in by_copies:
        copy.wait()
    wg_mid[...] = sum(wg_in[i].astype(F32) for i in range(COLS)).astype(BF16)
    for i, peer in enumerate(z_peers):
        copy = remote(wg_mid.at[peer], wg_col.at[z], b_s.at[i], b_r.at[i], ctx=col * PLANE + peer)
        copy.start()
        b_copies.append(copy)
    wg_col[z] = wg_mid[z]

    for i in range(PLANE):
        zc = lax.rem(z + 1 + i, PLANE)
        pack(col * PLANE + zc)
        if i < 2:
            mix_dkv(PLANE - 2 + i)
        dkvy_copies[i].wait_recv()
        mixed_copies[i].wait_recv()
        total = dkv_pack[col * PLANE + zc].astype(F32)
        for j in range(2):
            total = total + dkv_y[j, zc].astype(F32)
        if i == PLANE - 1:
            dkv_in[z] = total.astype(BF16)
        else:
            dkv_z[i] = total.astype(BF16)
            copy = remote(dkv_z.at[i], dkv_in.at[z], dkv_s.at[i], dkv_r.at[i], ctx=col * PLANE + zc)
            copy.start()
            dkv_copies.append(copy)
        if i == 1:
            for copy in b_copies:
                copy.wait()
            wg_last[...] = sum(wg_col[k].astype(F32) for k in range(PLANE)).astype(BF16)
            for k, peer in enumerate(dp_peers):
                copy = remote(wg_last, wg_all.at[dp], c_s.at[k], c_r.at[k], dp=peer)
                copy.start()
                c_copies.append(copy)
            wg_all[dp] = wg_last[...]

    for copy in dq_copies:
        copy.wait()
    for c in range(4):
        for half in range(2):
            dq_out[BLK * half:BLK * half + BLK, 128 * c:128 * c + 128] = pair_up(
                dq_all[2 * c], dq_all[2 * c + 1], half
            ).astype(BF16)

    for copy in c_copies:
        copy.wait()
    for c in range(4):
        even = wg_all[2 * c].astype(F32) + wg_all[PLANE + 2 * c].astype(F32)
        odd_ = wg_all[2 * c + 1].astype(F32) + wg_all[PLANE + 2 * c + 1].astype(F32)
        for half in range(2):
            wg_out[16 * half:16 * half + 16, 128 * c:128 * c + 128] = pair_up(even, odd_, half)

    for copy in dkv_copies:
        copy.wait()
    for c in range(4):
        for half in range(2):
            rows = slice(BLK * half, BLK * half + BLK)
            even, odd_ = dkv_in[2 * c, half], dkv_in[2 * c + 1, half]
            dkv_out[rows, 128 * c:128 * c + 128] = pair_up(even, odd_, 0).astype(BF16)
            dkv_out[rows, 512 + 128 * c:640 + 128 * c] = pair_up(even, odd_, 1).astype(BF16)

    for copy in (og_copies + og_core + q_copies + kv_copies + kvy_copies + dkvy_copies + far_copies
                 + mixed_copies + g_copies[1:] + o_copies[1:]):
        copy.wait_send()

    @pl.when(jnp.logical_not(here))
    def _():
        o_copies[0].wait_send()

    @pl.when(jnp.logical_not(stays))
    def _():
        g_copies[0].wait_send()


def table(block_list, counts, length, first):
    mine = lax.dynamic_slice_in_dim(block_list, first, UNITS, 0).reshape(ENTRIES)
    ids = jnp.arange(ENTRIES, dtype=jnp.int32)
    key = mine * ENTRIES + ids
    place = jnp.sum((key[None, :] < key[:, None]).astype(jnp.int32), axis=1)
    at = place[None, :] == ids[:, None]
    perm = jnp.sum(jnp.where(at, ids[None, :], 0), axis=1)
    same = (mine[None, :] == mine[:, None]) & (ids[None, :] < ids[:, None])
    later = jnp.max(same.astype(jnp.int32), axis=1)
    go_on = jnp.sum(jnp.where(at, later[None, :], 0), axis=1)
    blocks = jnp.arange(NQB, dtype=jnp.int32)
    upto = jnp.sum((mine[None, :] <= blocks[:, None]).astype(jnp.int32), axis=1)
    named = jnp.max((mine[None, :] == blocks[:, None]).astype(jnp.int32), axis=1)
    last = jnp.where(named > 0, upto - 1, ENTRIES)
    mine_counts = lax.dynamic_slice_in_dim(counts, first, UNITS, 0)
    return jnp.concatenate([mine, perm, go_on, last, mine_counts, length])


def per_device(queries, keyvals, out_weight, out_grad, block_lists, block_counts, seq_lengths):
    first = (lax.axis_index("ctx") // PLANE) * UNITS
    tab = table(block_lists[0], block_counts[0], seq_lengths, first)
    dma = pltpu.SemaphoreType.DMA
    vm = pltpu.VMEM
    hbm = pl.BlockSpec(memory_space=pltpu.HBM)
    zs, ys = PLANE - 1, COLS - 1
    pairs = [zs, ys, 3, 4, zs, zs, PLANE * ys, PLANE, PLANE, zs, PLANE * ys, zs, zs, ys, DP - 1]
    return pl.pallas_call(
        body,
        out_shape=(
            jax.ShapeDtypeStruct((128, 512), BF16),
            jax.ShapeDtypeStruct((128, 1024), BF16),
            jax.ShapeDtypeStruct((32, 512), F32),
        ),
        in_specs=[pl.BlockSpec(memory_space=pltpu.SMEM)] + [hbm] * 4,
        out_specs=tuple([pl.BlockSpec(memory_space=pltpu.VMEM)] * 3),
        scratch_shapes=[
            vm((128, 512), BF16), vm((128, 1024), BF16), vm((32, 512), BF16),
            vm((HEADS, 16, 128), BF16), vm((CTX, 16, 128), BF16),
            vm((PLANE, 128, 1024), BF16), vm((1024, 1024), BF16),
            vm((HEADS, BLK, 128), BF16), vm((PLANE, BLK, 128), BF16),
            vm((HEADS, 2, BLK, 128), BF16), vm((NQB, BLK, 128), BF16),
            vm((PLANE, BLK, 128), BF16), vm((PLANE, BLK, 128), BF16),
            vm((UNITS, BLK, KPQ * BLK), BF16),
            vm((PLANE, BLK, 128), BF16), vm((PLANE, BLK, 128), BF16),
            vm((PLANE, BLK, 128), BF16), vm((PLANE, BLK, 128), BF16),
            vm((ENTRIES, BLK, 128), F32), vm((ENTRIES + 1, BLK, 128), F32),
            vm((CTX, 2, BLK, 128), BF16), vm((COLS - 1, PLANE, 2, BLK, 128), BF16),
            vm((PLANE, 2, BLK, 128), BF16), vm((PLANE - 1, 2, BLK, 128), BF16),
            vm((HEADS, 2, BLK, 128), BF16),
            vm((COLS, PLANE, 16, 128), BF16), vm((COLS, PLANE, 16, 128), BF16),
            vm((PLANE, 16, 128), BF16), vm((PLANE, 16, 128), BF16),
            vm((16, 128), BF16), vm((DP, 16, 128), BF16),
            dma((4,)),
        ] + [dma((n,)) for n in pairs for _ in range(2)],
        compiler_params=pltpu.CompilerParams(
            collective_id=0, has_side_effects=True, vmem_limit_bytes=60 * 2**20
        ),
        name="attention_step",
    )(tab, queries, keyvals, out_weight, out_grad)


def solution(mesh):
    placed = (
        P(("dp", "ctx"), None),
        P(("dp", "ctx"), None),
        P("ctx", None),
        P(("dp", "ctx"), None),
        P("dp", None, None),
        P("dp", None),
        P("dp"),
    )
    return jax.shard_map(
        per_device,
        mesh=mesh,
        in_specs=placed,
        out_specs=(P(("dp", "ctx"), None), P(("dp", "ctx"), None), P("ctx", None)),
        check_vma=False,
    )
```
